256 devices in a mesh: doc: 32 (over z_lo, x, core), term: 8 (over y, z_hi).
Axes of the slice: x: 4, y: 4, z: 8 (z_hi: 2, z_lo: 4; z = z_hi * 4 + z_lo), core: 2. Of those that a mesh axis runs over, the one named last changes fastest.
Arguments:
- blocks: bfloat16 [32, 2560, 128, 128], P('doc', 'term'), may hold values from -6 to 6
- block_rows: int32 [32, 2560], P('doc', 'term'), may hold values from 0 to 63, as said below
- block_cols: int32 [32, 2560], P('doc', 'term'), may hold values from 0 to 63, as said below
- counts: int32 [32, 8], P('doc', 'term'), may hold values from 80 to 320, as said below
- start_panel: float32 [16, 65536], P(None, 'term'), may hold values from -6 to 6
Outputs:
- left_panel: float32 [16, 262144], P(None, 'doc')
- right_panel: float32 [16, 65536], P(None, 'term')
The draws below stay inside these ranges and needn't reach their ends.
Inputs may be any that keep to these rules, and one draw needn't show every extreme that they name: `block_rows`: within one tile the slots name distinct blocks. `block_cols`: within one tile the slots name distinct blocks. Some tile uses all 320 slots; slots from counts on are unused.
All inputs are finite; a program needn't handle non-finite values.
Results may differ from the reference program's by a relative error of at most 0.0092.
Values sent between devices are 32-bit elements; how exact they have to be, the bound alone decides.
No kernel may reach another device: no remote copies, remote signals or barrier semaphores. Data moves between devices by JAX's collectives and lax.ppermute only.
A program may use at most 64 MiB of HBM per device.

```python
import jax
import jax.numpy as jnp
from jax import lax

BLK = 128
K = 16
BR = 64
BC = 64
NB = 320
ITERS = 2
DOCS = 262144
TERMS = 65536
N_DOC = 32
N_TERM = 8


def block_positions(key):
    keys = jax.random.split(jax.random.fold_in(key, 11), N_DOC * N_TERM)
    chosen = jax.vmap(lambda single: jax.random.permutation(single, BR * BC)[:NB])(keys)
    return chosen.reshape(N_DOC, N_TERM * NB).astype(jnp.int32)


def draw_block_rows(key, part):
    return (block_positions(key) // BC).astype(jnp.int32)


def draw_block_cols(key, part):
    return (block_positions(key) % BC).astype(jnp.int32)


def draw_counts(key, part):
    divisor = jax.random.randint(jax.random.fold_in(key, 5), (N_DOC * N_TERM,), 1, 5)
    filled = NB // divisor
    picked = jax.random.randint(jax.random.fold_in(key, 3), (), 0, N_DOC * N_TERM)
    filled = filled.at[picked].set(NB)
    return filled.reshape(N_DOC, N_TERM).astype(jnp.int32)


def steps_of(key, shape, cuts, low, largest):
    factor_of, own = 1.0, jax.random.fold_in(key, 6)
    for dim, blocks in cuts:
        draws = jnp.exp(jax.random.uniform(jax.random.fold_in(own, dim), (blocks,), jnp.float32, low / len(cuts), largest / len(cuts)))
        factor_of = factor_of * jnp.repeat(draws, shape[dim] // blocks).reshape([-1 if axis == dim else 1 for axis in range(len(shape))])
    return factor_of


def bell_draw(key, dims, width, reach, cuts=(), held_as=jnp.bfloat16):
    values = jax.random.normal(key, dims, jnp.float32) * width
    if len(cuts) > 0:
        values = steps_of(key, dims, cuts, -0.22, 0.18) * values
    return jnp.clip(values, min=-reach, max=reach).astype(held_as)


def setup_inputs(seed: int = 0) -> dict:
    streams_of = jax.random.split(jax.random.key(seed), 6)
    blocks = bell_draw(streams_of[0], (N_DOC, N_TERM * NB, BLK, BLK), 1.0, 6.0, ((0, 32), (1, 8)))
    block_rows = draw_block_rows(jax.random.fold_in(streams_of[5], 71), 0)
    block_cols = draw_block_cols(jax.random.fold_in(streams_of[5], 71), 0)
    counts = draw_counts(jax.random.fold_in(streams_of[5], 71), 0)
    start_panel = bell_draw(streams_of[4], (K, TERMS), 1.0, 6.0, ((1, 8),), jnp.float32)
    return {"blocks": blocks, "block_rows": block_rows, "block_cols": block_cols, "counts": counts, "start_panel": start_panel}


def orthonormal(block_in, prior, count_all):
    hp = lax.Precision.HIGHEST
    if prior is None:
        projected = block_in
    else:
        coeffs = jnp.dot(block_in, prior.T, precision=hp) / count_all
        projected = block_in - jnp.dot(coeffs, prior, precision=hp)
    gram = jnp.dot(projected, projected.T, precision=hp) / count_all
    factor = jnp.linalg.cholesky(gram)
    return lax.linalg.triangular_solve(factor, projected, left_side=True, lower=True)

def slot_layout(cols_doc, counts_doc):
    slot_ids = jnp.arange(N_TERM * NB, dtype=jnp.int32)
    term_of = slot_ids // NB
    global_cols = (term_of * BC + cols_doc).astype(jnp.int32)
    live = slot_ids % NB < counts_doc[term_of]
    return (global_cols, live)

def forward_product(blocks, block_rows, block_cols, counts, right_bf):
    pieces = right_bf.reshape(K, N_TERM * BC, BLK)

    def one_doc(packed):
        tile_blocks, rows_doc, cols_doc, counts_doc = packed
        global_cols, live = slot_layout(cols_doc, counts_doc)
        gathered = jnp.take(pieces, global_cols, axis=1).astype(jnp.float32)
        products = jnp.einsum('nrc,knc->nkr', tile_blocks.astype(jnp.float32), gathered)
        products = products * live[:, None, None].astype(jnp.float32)
        summed = jax.ops.segment_sum(products, rows_doc, num_segments=BR)
        return jnp.transpose(summed, (1, 0, 2)).reshape(K, BR * BLK)
    result = lax.map(one_doc, (blocks, block_rows, block_cols, counts))
    return jnp.transpose(result, (1, 0, 2)).reshape(K, DOCS)

def backward_product(blocks, block_rows, block_cols, counts, left_bf):
    pieces = left_bf.reshape(K, N_DOC, BR, BLK)

    def one_doc(total, packed):
        tile_blocks, rows_doc, cols_doc, counts_doc, doc_piece = packed
        global_cols, live = slot_layout(cols_doc, counts_doc)
        gathered = jnp.take(doc_piece, rows_doc, axis=1).astype(jnp.float32)
        products = jnp.einsum('nrc,knr->nkc', tile_blocks.astype(jnp.float32), gathered)
        products = products * live[:, None, None].astype(jnp.float32)
        return (total + jax.ops.segment_sum(products, global_cols, num_segments=N_TERM * BC), None)
    start_total = jnp.zeros((N_TERM * BC, K, BLK), jnp.float32)
    doc_pieces = jnp.transpose(pieces, (1, 0, 2, 3))
    total, unused = lax.scan(one_doc, start_total, (blocks, block_rows, block_cols, counts, doc_pieces))
    return jnp.transpose(total, (1, 0, 2)).reshape(K, TERMS)

def reference(blocks, block_rows, block_cols, counts, start_panel):
    right_panel = orthonormal(start_panel, None, TERMS)
    left_panel = None
    for sweep in range(ITERS):
        right_bf = right_panel.astype(jnp.bfloat16)
        forward = forward_product(blocks, block_rows, block_cols, counts, right_bf)
        left_panel = orthonormal(forward, left_panel, DOCS)
        left_bf = left_panel.astype(jnp.bfloat16)
        backward = backward_product(blocks, block_rows, block_cols, counts, left_bf)
        right_panel = orthonormal(backward, right_panel, TERMS)
    return (left_panel, right_panel)
```

```python
import functools

import jax
import jax.numpy as jnp
import numpy as np
from jax import lax
from jax.experimental import pallas as pl
from jax.experimental.pallas import tpu as pltpu
from jax.sharding import Mesh
from jax.sharding import PartitionSpec as P

BLK = 128
K = 16
BR = 64
NB = 320
CHUNK = 32
UNROLL = 8
DOC = ("zl", "x", "c")
TERM = ("y", "zh")
F32 = jnp.float32
BF = jnp.bfloat16
HI = lax.Precision.HIGHEST
VMEM = pltpu.VMEM
SMEM = pltpu.SMEM


def mm(a, b):
    return jnp.dot(a, b, precision=HI, preferred_element_type=F32)


def mmt(a, b):
    return lax.dot_general(a, b, (((1,), (1,)), ((), ())), precision=HI, preferred_element_type=F32)


def inverse_factor(gram):
    lane = lax.broadcasted_iota(jnp.int32, (K, BLK), 1)
    row = lax.broadcasted_iota(jnp.int32, (K, BLK), 0)
    aug = jnp.concatenate([gram, jnp.zeros((K, BLK - K), F32)], axis=1)
    aug = jnp.where(lane == row + K, 1.0, aug)
    for j in range(K - 1):
        pivot_row = aug[j : j + 1, :]
        ratio = pivot_row / pivot_row[:, j : j + 1]
        aug = aug - jnp.where(row > j, aug[:, j : j + 1], 0.0) * ratio
    diag = jnp.sum(jnp.where(lane == row, aug, 0.0), axis=1, keepdims=True)
    return aug[:, K : 2 * K] * lax.rsqrt(diag)


def columns(matrix):
    return [jnp.broadcast_to(matrix[:, j : j + 1], (K, BLK)) for j in range(K)]


def combine(cols, piece):
    total = cols[0] * piece[0:1, :]
    for j in range(1, K):
        total = total + cols[j] * piece[j : j + 1, :]
    return total


def split_store(split_ref, index, value):
    high = value.astype(BF)
    rest = value - high.astype(F32)
    middle = rest.astype(BF)
    low = (rest - middle.astype(F32)).astype(BF)
    split_ref[index, 0:16, :] = high
    split_ref[index, 16:32, :] = middle
    split_ref[index, 32:48, :] = low


def fold(wide):
    rows = (wide[32:48, :] + wide[16:32, :]) + wide[0:16, :]
    return (rows[:, 32:48] + rows[:, 16:32]) + rows[:, 0:16]


def gram_of(left_ref, right_ref, count=BR):
    def step(i, total):
        return total + lax.dot_general(
            left_ref[i], right_ref[i], (((1,), (1,)), ((), ())), preferred_element_type=F32
        )

    return fold(lax.fori_loop(0, count, step, jnp.zeros((48, 48), F32), unroll=8))


def pad_lanes(*parts):
    width = sum(p.shape[1] for p in parts)
    return jnp.concatenate([*parts, jnp.zeros((K, BLK - width), F32)], axis=1)


def start_copies(blocks_ref, held, sems):
    for i in range(NB // CHUNK):
        part = pl.ds(i * CHUNK, CHUNK)
        pltpu.make_async_copy(blocks_ref.at[0, part], held.at[part], sems.at[i]).start()


def multiply(scal, src_ref, tgt_ref, blocks_ref, held, sems, split, acc, place, spare, forward):
    acc[...] = jnp.zeros_like(acc)
    live = scal[0]
    dims = (((1,), (1,)), ((), ())) if forward else (((1,), (0,)), ((), ()))

    def chunk_step(i, carry):
        part = pl.ds(i * CHUNK, CHUNK)
        pltpu.make_async_copy(blocks_ref.at[0, part], held.at[part], sems.at[i]).wait()
        left = jnp.clip(live - i * CHUNK, 0, CHUNK)
        groups = lax.div(left + (UNROLL - 1), UNROLL)

        def group_step(g, inner):
            base = i * CHUNK + g * UNROLL
            places, values = [], []
            for u in range(UNROLL):
                slot = base + u
                wide = lax.dot_general(
                    split[src_ref[0, slot]], held[slot], dims, preferred_element_type=F32
                )
                values.append((wide[32:48, :] + wide[16:32, :]) + wide[0:16, :])
                places.append(jnp.where(slot < live, place(tgt_ref[0, slot]), spare))
            for where_to, value in zip(places, values):
                acc[where_to] += value
            return inner

        lax.fori_loop(0, groups, group_step, 0)
        return carry

    lax.fori_loop(0, NB // CHUNK, chunk_step, 0)


def term_place(target):
    return lax.shift_right_logical(target, 4) * 17 + jnp.bitwise_and(target, 15)


def doc_place(core):
    def place(target):
        half = jnp.bitwise_xor(lax.shift_right_logical(target, 5), core)
        quarter = jnp.bitwise_and(lax.shift_right_logical(target, 3), 3)
        return half * 36 + quarter * 9 + jnp.bitwise_and(target, 7)

    return place


def first_forward(scal, rows, cols, start, blocks, acc, held, sems, split):
    start_copies(blocks, held, sems)
    for i in range(BR):
        split_store(split, i, start[:, i * BLK : (i + 1) * BLK])
    ext = pad_lanes(gram_of(split, split))
    multiply(scal, cols, rows, blocks, held, sems, split, acc, term_place, 16, True)
    for j in range(4):
        acc[j * 17 + 16] = ext


def first_backward(
    scal, rows, cols, summed, ext, blocks, own, other, left_raw, mr0, held, sems, split, acc, *, terms
):
    start_copies(blocks, held, sems)
    inverse = inverse_factor(ext[:, 0:K] / terms)
    mr0[...] = pad_lanes(inverse)
    cols_m = columns(inverse)

    def step(i, carry):
        value = combine(cols_m, summed[i])
        left_raw[i] = value
        split_store(split, i, value)
        return carry

    lax.fori_loop(0, BR, step, 0, unroll=2)
    out = pad_lanes(gram_of(split, split))
    multiply(scal, rows, cols, blocks, held, sems, split, acc, doc_place(scal[1]), 8, False)
    for j in range(8):
        acc[j * 9 + 8] = out
    own[...] = acc[0:36]
    other[...] = acc[36:72]


def second_forward(
    scal, rows, cols, mine, theirs, ext, start, mr0, blocks, acc, right_raw, right0, ml1,
    held, sems, split, split0, *, docs
):
    start_copies(blocks, held, sems)
    core = scal[1]
    inverse = inverse_factor(ext[:, 0:K] / docs)
    ml1[...] = pad_lanes(inverse)
    cols_m = columns(inverse)

    def half(source, base):
        def step(i, carry):
            value = combine(cols_m, source[i])
            right_raw[base + i] = value
            split_store(split, base + i, value)
            return carry

        lax.fori_loop(0, BR // 2, step, 0, unroll=2)

    half(mine, core * 32)
    half(theirs, (1 - core) * 32)
    cols_0 = columns(mr0[:, 0:K])
    for i in range(BR):
        value = combine(cols_0, start[:, i * BLK : (i + 1) * BLK])
        right0[i] = value
        split_store(split0, i, value)
    out = pad_lanes(gram_of(split, split), gram_of(split, split0))
    multiply(scal, cols, rows, blocks, held, sems, split, acc, term_place, 16, True)
    for j in range(4):
        acc[j * 17 + 16] = out


def second_backward(
    scal, rows, cols, summed, ext, left_raw, ml1, blocks, own, other, left2_raw, left1, mr1, mh,
    held, sems, split, split1, acc, *, terms
):
    start_copies(blocks, held, sems)
    proj = ext[:, K : 2 * K] / terms
    inverse = inverse_factor(ext[:, 0:K] / terms - mmt(proj, proj))
    both = mm(inverse, proj)
    mr1[...] = pad_lanes(inverse)
    mh[...] = pad_lanes(both)
    cols_l = columns(ml1[:, 0:K])

    def left_step(i, carry):
        value = combine(cols_l, left_raw[i])
        left1[i] = value
        split_store(split1, i, value)
        return carry

    lax.fori_loop(0, BR, left_step, 0, unroll=2)
    cols_b = columns(both)

    def back_step(i, carry):
        left2_raw[i] = combine(cols_b, left_raw[i])
        return carry

    lax.fori_loop(0, BR, back_step, 0, unroll=2)
    cols_m = columns(inverse)

    def step(i, carry):
        value = combine(cols_m, summed[i]) - left2_raw[i]
        left2_raw[i] = value
        split_store(split, i, value)
        return carry

    lax.fori_loop(0, BR, step, 0, unroll=2)
    out = pad_lanes(gram_of(split, split), gram_of(split, split1))
    multiply(scal, rows, cols, blocks, held, sems, split, acc, doc_place(scal[1]), 8, False)
    for j in range(8):
        acc[j * 9 + 8] = out
    own[...] = acc[0:36]
    other[...] = acc[36:72]


def last_left(
    scal, mine, theirs, ext, left2_raw, left1, right_raw, right0, mr1, mh,
    left_out, right2_raw, right1, ext_out, split, split1, *, docs
):
    core = scal[1]
    proj = ext[:, K : 2 * K] / docs
    inverse = inverse_factor(ext[:, 0:K] / docs - mmt(proj, proj))
    both = mm(inverse, proj)
    cols_b = columns(both)
    for i in range(BR):
        left_out[:, i * BLK : (i + 1) * BLK] = combine(cols_b, left1[i])
    cols_r = columns(mh[:, 0:K])

    def right_step(i, carry):
        right1[i] = combine(cols_r, right0[i])
        right2_raw[i] = combine(cols_b, right_raw[i])
        return carry

    lax.fori_loop(0, BR, right_step, 0)
    cols_1 = columns(mr1[:, 0:K])

    def right1_step(i, carry):
        value = combine(cols_1, right_raw[i]) - right1[i]
        right1[i] = value
        split_store(split1, i, value)
        return carry

    lax.fori_loop(0, BR, right1_step, 0, unroll=2)
    cols_m = columns(inverse)

    def half(source, base):
        def step(i, carry):
            value = combine(cols_m, source[i]) - right2_raw[base + i]
            right2_raw[base + i] = value
            split_store(split, base + i, value)
            return carry

        lax.fori_loop(0, BR // 2, step, 0, unroll=2)

    half(mine, core * 32)
    half(theirs, (1 - core) * 32)
    for i in range(BR):
        part = slice(i * BLK, (i + 1) * BLK)
        left_out[:, part] = combine(cols_m, left2_raw[i]) - left_out[:, part]
    ext_out[...] = pad_lanes(gram_of(split, split), gram_of(split, split1))


def last_right(ext, right2_raw, right1, right_out, *, terms):
    proj = ext[:, K : 2 * K] / terms
    inverse = inverse_factor(ext[:, 0:K] / terms - mmt(proj, proj))
    cols_b = columns(mm(inverse, proj))
    for i in range(BR):
        right_out[:, i * BLK : (i + 1) * BLK] = combine(cols_b, right1[i])
    cols_m = columns(inverse)
    for i in range(BR):
        part = slice(i * BLK, (i + 1) * BLK)
        right_out[:, part] = combine(cols_m, right2_raw[i]) - right_out[:, part]


def panel(n=BR):
    return jax.ShapeDtypeStruct((n, K, BLK), F32)


SMALL = jax.ShapeDtypeStruct((K, BLK), F32)
WIDE = jax.ShapeDtypeStruct((K, BR * BLK), F32)
HELD = [VMEM((NB, BLK, BLK), BF), pltpu.SemaphoreType.DMA((NB // CHUNK,))]
SPLIT = VMEM((BR, 48, BLK), BF)


def call(body, name, args, outs, scratch, product=True):
    in_specs = []
    for i, a in enumerate(args):
        if product and i == len(args) - 1:
            in_specs.append(pl.BlockSpec(memory_space=pl.ANY))
        else:
            integer = a.dtype == jnp.int32
            in_specs.append(pl.BlockSpec(memory_space=SMEM if integer else VMEM))
    return pl.pallas_call(
        body,
        name=name,
        out_shape=outs,
        in_specs=in_specs,
        out_specs=jax.tree.map(lambda _: pl.BlockSpec(memory_space=VMEM), outs),
        scratch_shapes=scratch,
        compiler_params=pltpu.CompilerParams(vmem_limit_bytes=48 * 1024 * 1024),
    )(*args)


SWAP = [(0, 1), (1, 0)]


def copies(value):
    return jnp.broadcast_to(value[None], (4, *value.shape))


def sum_term(acc):
    parts = lax.all_to_all(acc.reshape(4, 17, K, BLK), "y", 0, 0)
    total = ((parts[0] + parts[1]) + parts[2]) + parts[3]
    total = total + lax.ppermute(total, "zh", SWAP)
    full = lax.all_to_all(copies(total[:16]), "y", 0, 0)
    return full.reshape(BR, K, BLK), total[16]


def sum_doc(own, other):
    total = own + lax.ppermute(other, "c", SWAP)
    for axis in ("x", "zl"):
        send = total.reshape(4, 9, K, BLK) if axis == "x" else copies(total)
        parts = lax.all_to_all(send, axis, 0, 0)
        total = ((parts[0] + parts[1]) + parts[2]) + parts[3]
    mine = lax.all_to_all(copies(total[:8]), "x", 0, 0).reshape(BR // 2, K, BLK)
    return mine, lax.ppermute(mine, "c", SWAP), total[8]


def local(blocks, block_rows, block_cols, counts, start):
    core = lax.axis_index("c").astype(jnp.int32)
    scal = jnp.stack([counts[0, 0], core])
    docs = float(BR * BLK * 32)
    terms = float(BR * BLK * 8)
    index = (scal, block_rows, block_cols)

    acc = call(first_forward, "first_forward", (*index, start, blocks), panel(68), [*HELD, SPLIT])
    summed, ext = sum_term(acc)
    own, other, left_raw, mr0 = call(
        functools.partial(first_backward, terms=terms),
        "first_backward",
        (*index, summed, ext, blocks),
        (panel(36), panel(36), panel(), SMALL),
        [*HELD, SPLIT, VMEM((72, K, BLK), F32)],
    )
    mine, theirs, ext = sum_doc(own, other)
    acc, right_raw, right0, ml1 = call(
        functools.partial(second_forward, docs=docs),
        "second_forward",
        (*index, mine, theirs, ext, start, mr0, blocks),
        (panel(68), panel(), panel(), SMALL),
        [*HELD, SPLIT, SPLIT],
    )
    summed, ext = sum_term(acc)
    own, other, left2_raw, left1, mr1, mh = call(
        functools.partial(second_backward, terms=terms),
        "second_backward",
        (*index, summed, ext, left_raw, ml1, blocks),
        (panel(36), panel(36), panel(), panel(), SMALL, SMALL),
        [*HELD, SPLIT, SPLIT, VMEM((72, K, BLK), F32)],
    )
    mine, theirs, ext = sum_doc(own, other)
    left_out, right2_raw, right1, ext = call(
        functools.partial(last_left, docs=docs),
        "last_left",
        (scal, mine, theirs, ext, left2_raw, left1, right_raw, right0, mr1, mh),
        (WIDE, panel(), panel(), SMALL),
        [SPLIT, SPLIT],
        product=False,
    )
    ext = jnp.sum(lax.all_to_all(jnp.broadcast_to(ext[None], (8, K, BLK)), TERM, 0, 0), axis=0)
    right_out = call(
        functools.partial(last_right, terms=terms),
        "last_right",
        (ext, right2_raw, right1),
        WIDE,
        [],
        product=False,
    )
    return left_out, right_out


def solution(mesh):
    fine = Mesh(
        np.asarray(mesh.devices).reshape(4, 4, 2, 4, 2), (*DOC, *TERM)
    )
    return jax.shard_map(
        local,
        mesh=fine,
        in_specs=(P(DOC, TERM, None, None), P(DOC, TERM), P(DOC, TERM), P(DOC, TERM), P(None, TERM)),
        out_specs=(P(None, DOC), P(None, TERM)),
        check_vma=False,
    )
```

```python
import functools

import jax
import jax.numpy as jnp
import numpy as np
from jax import lax
from jax.experimental import pallas as pl
from jax.experimental.pallas import tpu as pltpu
from jax.sharding import Mesh
from jax.sharding import PartitionSpec as P

BLK = 128
K = 16
BR = 64
NB = 320
GROUP = 32
DOC = ("zl", "x", "c")
TERM = ("y", "zh")
F32 = jnp.float32
BF = jnp.bfloat16
HI = lax.Precision.HIGHEST
VMEM = pltpu.VMEM
SMEM = pltpu.SMEM
ANY = pl.ANY


def mm(a, b):
    return jnp.dot(a, b, precision=HI, preferred_element_type=F32)


def mmt(a, b):
    return lax.dot_general(a, b, (((1,), (1,)), ((), ())), precision=HI, preferred_element_type=F32)


def inverse_factor(gram):
    lane = lax.broadcasted_iota(jnp.int32, (K, BLK), 1)
    row = lax.broadcasted_iota(jnp.int32, (K, BLK), 0)
    aug = jnp.concatenate([gram, jnp.zeros((K, BLK - K), F32)], axis=1)
    aug = jnp.where(lane == row + K, 1.0, aug)
    for j in range(K - 1):
        pivot_row = aug[j : j + 1, :]
        ratio = pivot_row / pivot_row[:, j : j + 1]
        aug = aug - jnp.where(row > j, aug[:, j : j + 1], 0.0) * ratio
    diag = jnp.sum(jnp.where(lane == row, aug, 0.0), axis=1, keepdims=True)
    return aug[:, K : 2 * K] * lax.rsqrt(diag)


def projected(ext, count):
    proj = ext[:, K : 2 * K] / count
    return proj, inverse_factor(ext[:, 0:K] / count - mmt(proj, proj))


def columns(matrix):
    return [jnp.broadcast_to(matrix[:, j : j + 1], (K, BLK)) for j in range(K)]


def combine(cols, piece):
    total = cols[0] * piece[0:1, :]
    for j in range(1, K):
        total = total + cols[j] * piece[j : j + 1, :]
    return total


def parts(value):
    high = value.astype(BF)
    rest = value - high.astype(F32)
    middle = rest.astype(BF)
    low = (rest - middle.astype(F32)).astype(BF)
    return high, middle, low


def stacked(value):
    return jnp.concatenate(parts(value), axis=0)


def split_store(split_ref, index, value):
    high, middle, low = parts(value)
    split_ref[index, 0:16, :] = high
    split_ref[index, 16:32, :] = middle
    split_ref[index, 32:48, :] = low


def cross(left, right):
    return lax.dot_general(left, right, (((1,), (1,)), ((), ())), preferred_element_type=F32)


def fold(wide):
    rows = (wide[32:48, :] + wide[16:32, :]) + wide[0:16, :]
    return (rows[:, 32:48] + rows[:, 16:32]) + rows[:, 0:16]


def pad_lanes(*pieces):
    width = sum(p.shape[1] for p in pieces)
    return jnp.concatenate([*pieces, jnp.zeros((K, BLK - width), F32)], axis=1)


def spin(index, step):
    return jnp.bitwise_and(index - step, 3)


def group_of(base, live, src_ref, tgt_ref, block, split, acc, place, spare):
    spots, values = [], []
    for u in range(GROUP):
        slot = base + u
        wide = jnp.dot(split[src_ref[0, slot]], block(slot), preferred_element_type=F32)
        values.append((wide[32:48, :] + wide[16:32, :]) + wide[0:16, :])
        spots.append(jnp.where(slot < live, place(tgt_ref[0, slot]), spare))
    for spot, value in zip(spots, values):
        acc[spot] += value


def term_place(y):
    def place(target):
        part = jnp.bitwise_and(lax.shift_right_logical(target, 4) - y, 3)
        return part * 17 + jnp.bitwise_and(target, 15)

    return place


def doc_place(x, core):
    def place(target):
        half = jnp.bitwise_xor(lax.shift_right_logical(target, 5), core)
        part = jnp.bitwise_and(lax.shift_right_logical(target, 3) - x, 3)
        return half * 36 + part * 9 + jnp.bitwise_and(target, 7)

    return place


def multiply(live, src_ref, tgt_ref, held, split, acc, place, spare):
    def step(g, carry):
        group_of(g * GROUP, live, src_ref, tgt_ref, lambda s: held[s], split, acc, place, spare)
        return carry

    lax.fori_loop(0, lax.div(live + (GROUP - 1), GROUP), step, 0)


def first_forward(
    rows_any, cols_any, counts_any, start, blocks, o0, o1, o2, o3, held, turned,
    rows, cols, counts, split, acc, sems, small_sems,
):
    groups = NB // GROUP
    small = [
        pltpu.make_async_copy(rows_any, rows, small_sems.at[0]),
        pltpu.make_async_copy(cols_any, cols, small_sems.at[1]),
        pltpu.make_async_copy(counts_any, counts, small_sems.at[2]),
    ]
    for copy in small:
        copy.start()
    for i in range(groups):
        part = pl.ds(i * GROUP, GROUP)
        pltpu.make_async_copy(blocks.at[0, part], held.at[part], sems.at[i]).start()
    acc[...] = jnp.zeros_like(acc)
    gram = jnp.zeros((48, 48), F32)
    for i in range(BR):
        value = stacked(start[:, i * BLK : (i + 1) * BLK])
        split[i] = value
        gram = gram + cross(value, value)
    ext = pad_lanes(fold(gram))
    for copy in small:
        copy.wait()
    live = counts[0, 0]
    place = term_place(lax.axis_index("y"))

    def turn(slot):
        value = held[slot].T
        turned[slot] = value
        return value

    def step(i, carry):
        part = pl.ds(i * GROUP, GROUP)
        pltpu.make_async_copy(blocks.at[0, part], held.at[part], sems.at[i]).wait()

        @pl.when(i * GROUP < live)
        def _():
            group_of(i * GROUP, live, cols, rows, turn, split, acc, place, 16)

        return carry

    lax.fori_loop(0, groups, step, 0)
    for k, out in enumerate((o0, o1, o2, o3)):
        out[0:16] = acc[k * 17 : k * 17 + 16]
        out[16] = ext


def forward(rows, cols, counts, r0, r1, r2, r3, w0, w1, w2, w3, turned, o0, o1, o2, o3, split, acc, grams):
    x, core = lax.axis_index("x"), lax.axis_index("c")
    acc[...] = jnp.zeros_like(acc)
    for side, pieces in ((core, (r0, r1, r2, r3)), (1 - core, (w0, w1, w2, w3))):
        for k, piece in enumerate(pieces):
            base = side * 32 + spin(x, k) * 8
            for i in range(8):
                split_store(split, base + i, piece[i])
            grams[side * 4 + spin(x, k)] = piece[8]
    multiply(counts[0, 0], cols, rows, turned, split, acc, term_place(lax.axis_index("y")), 16)
    ext = grams[0]
    for i in range(1, 8):
        ext = ext + grams[i]
    for k, out in enumerate((o0, o1, o2, o3)):
        out[0:16] = acc[k * 17 : k * 17 + 16]
        out[16] = ext


def backward(rows, cols, counts, p0, p1, p2, p3, held, own, other, split, acc, grams):
    y = lax.axis_index("y")
    acc[...] = jnp.zeros_like(acc)
    for k, piece in enumerate((p0, p1, p2, p3)):
        base = spin(y, k) * 16
        for i in range(16):
            split_store(split, base + i, piece[i])
        grams[spin(y, k)] = piece[16]
    place = doc_place(lax.axis_index("x"), lax.axis_index("c"))
    multiply(counts[0, 0], rows, cols, held, split, acc, place, 8)
    ext = ((grams[0] + grams[1]) + grams[2]) + grams[3]
    for j in range(8):
        acc[j * 9 + 8] = ext
    own[...] = acc[0:36]
    other[...] = acc[36:72]


def left_first(mine, theirs, out, mr0, *, terms):
    inverse = inverse_factor((mine[16] + theirs[16])[:, 0:K] / terms)
    mr0[...] = pad_lanes(inverse)
    cols = columns(inverse)
    gram = jnp.zeros((48, 48), F32)
    for i in range(16):
        value = combine(cols, mine[i] + theirs[i])
        out[i] = value
        wide = stacked(value)
        gram = gram + cross(wide, wide)
    out[16] = pad_lanes(fold(gram))


def zl_total(t0, t1, t2, t3, order):
    zl = lax.axis_index("zl")
    for k, piece in enumerate((t0, t1, t2, t3)):
        order[spin(zl, k)] = piece[...]
    return lambda i: ((order[0, i] + order[1, i]) + order[2, i]) + order[3, i]


def right_first(t0, t1, t2, t3, start, mr0, out, ml1, right0, order, *, docs):
    total = zl_total(t0, t1, t2, t3, order)
    x, core = lax.axis_index("x"), lax.axis_index("c")
    first = (core * 32 + x * 8) * BLK
    inverse = inverse_factor(total(8)[:, 0:K] / docs)
    ml1[...] = pad_lanes(inverse)
    cols_0 = columns(mr0[:, 0:K])
    cols_1 = columns(inverse)
    gram = jnp.zeros((48, 48), F32)
    mixed = jnp.zeros((48, 48), F32)
    for i in range(8):
        source = pl.ds(pl.multiple_of(first + i * BLK, BLK), BLK)
        prior = combine(cols_0, start[:, source])
        right0[i] = prior
        value = combine(cols_1, total(i))
        out[i] = value
        wide = stacked(value)
        gram = gram + cross(wide, wide)
        mixed = mixed + cross(wide, stacked(prior))
    out[8] = pad_lanes(fold(gram), fold(mixed))


def left_second(mine, theirs, left_raw, ml1, out, mr1, h1, *, terms):
    proj, inverse = projected(mine[16] + theirs[16], terms)
    mr1[...] = pad_lanes(inverse)
    h1[...] = pad_lanes(proj)
    cols_l = columns(ml1[:, 0:K])
    cols_h = columns(proj)
    for i in range(16):
        out[i] = (mine[i] + theirs[i]) - combine(cols_h, left_raw[i])
    cols_m = columns(inverse)
    gram = jnp.zeros((48, 48), F32)
    mixed = jnp.zeros((48, 48), F32)
    for i in range(16):
        prior = stacked(combine(cols_l, left_raw[i]))
        value = combine(cols_m, out[i])
        out[i] = value
        wide = stacked(value)
        gram = gram + cross(wide, wide)
        mixed = mixed + cross(wide, prior)
    out[16] = pad_lanes(fold(gram), fold(mixed))


def right_second(t0, t1, t2, t3, right_raw, right0, mr1, h1, out, ext_out, ml2, h2, order, prior, *, docs):
    cols_0 = columns(h1[:, 0:K])
    cols_1 = columns(mr1[:, 0:K])
    for i in range(8):
        prior[i] = stacked(combine(cols_1, right_raw[i] - combine(cols_0, right0[i])))
    total = zl_total(t0, t1, t2, t3, order)
    proj, inverse = projected(total(8), docs)
    ml2[...] = pad_lanes(inverse)
    h2[...] = pad_lanes(proj)
    cols_h = columns(proj)
    for i in range(8):
        out[i] = total(i) - combine(cols_h, right_raw[i])
    cols_m = columns(inverse)
    gram = jnp.zeros((48, 48), F32)
    mixed = jnp.zeros((48, 48), F32)
    for i in range(8):
        value = combine(cols_m, out[i])
        out[i] = value
        wide = stacked(value)
        gram = gram + cross(wide, wide)
        mixed = mixed + cross(wide, prior[i])
    ext_out[...] = pad_lanes(fold(gram), fold(mixed))


def left_result(a0, a1, a2, a3, b0, b1, b2, b3, ml1, ml2, h2, out):
    y = lax.axis_index("y")
    inverse = ml2[:, 0:K]
    for k, (first, second) in enumerate(zip((a0, a1, a2, a3), (b0, b1, b2, b3))):
        base = spin(y, k) * 16

        def part(i):
            return pl.ds(pl.multiple_of((base + i) * BLK, BLK), BLK)

        cols = columns(ml1[:, 0:K])
        for i in range(16):
            out[:, part(i)] = combine(cols, first[i])
        cols = columns(h2[:, 0:K])
        for i in range(16):
            out[:, part(i)] = second[i] - combine(cols, out[:, part(i)])
        cols = columns(inverse)
        for i in range(16):
            out[:, part(i)] = combine(cols, out[:, part(i)])


def right_prior(r0, r1, r2, r3, w0, w1, w2, w3, start, mr0, mr1, h1, out):
    x, core = lax.axis_index("x"), lax.axis_index("c")

    def each(cols_of, update):
        cols = columns(cols_of[:, 0:K])
        for i in range(BR):
            update(cols, i)

    def from_start(cols, i):
        out[i] = combine(cols, start[:, i * BLK : (i + 1) * BLK])

    def times_h(cols, i):
        out[i] = combine(cols, out[i])

    each(mr0, from_start)
    each(h1, times_h)
    cols = columns(mr1[:, 0:K])
    for side, pieces in ((core, (r0, r1, r2, r3)), (1 - core, (w0, w1, w2, w3))):
        for k, piece in enumerate(pieces):
            base = side * 32 + spin(x, k) * 8
            for i in range(8):
                out[base + i] = combine(cols, piece[i] - out[base + i])


def right_result(ext, r0, r1, r2, r3, w0, w1, w2, w3, right1, out, *, terms):
    x, core = lax.axis_index("x"), lax.axis_index("c")
    total = ext[0]
    for i in range(1, ext.shape[0]):
        total = total + ext[i]
    proj, inverse = projected(total, terms)
    spots = []
    for side, pieces in ((core, (r0, r1, r2, r3)), (1 - core, (w0, w1, w2, w3))):
        for k, piece in enumerate(pieces):
            spots += [(side * 32 + spin(x, k) * 8 + i, piece, i) for i in range(8)]

    def part(spot):
        return pl.ds(pl.multiple_of(spot * BLK, BLK), BLK)

    cols = columns(proj)
    for spot, piece, i in spots:
        out[:, part(spot)] = piece[i] - combine(cols, right1[spot])
    cols = columns(inverse)
    for spot, piece, i in spots:
        out[:, part(spot)] = combine(cols, out[:, part(spot)])


def panel(n):
    return jax.ShapeDtypeStruct((n, K, BLK), F32)


SMALL = jax.ShapeDtypeStruct((K, BLK), F32)
WIDE = jax.ShapeDtypeStruct((K, BR * BLK), F32)
TILE = jax.ShapeDtypeStruct((NB, BLK, BLK), BF)
SPLIT = VMEM((BR, 48, BLK), BF)


def held_panel(n):
    return VMEM((n, K, BLK), F32)


def call(body, args, outs, scratch=(), spaces=None, limit=8, **constants):
    def space(a):
        return SMEM if a.dtype == jnp.int32 else VMEM

    spaces = spaces or [space(a) for a in args]
    return pl.pallas_call(
        functools.partial(body, **constants) if constants else body,
        name=body.__name__,
        out_shape=outs,
        in_specs=[pl.BlockSpec(memory_space=s) for s in spaces],
        out_specs=jax.tree.map(lambda _: pl.BlockSpec(memory_space=VMEM), outs),
        scratch_shapes=list(scratch),
        compiler_params=pltpu.CompilerParams(vmem_limit_bytes=limit * 1024 * 1024),
    )(*args)


SWAP = [(0, 1), (1, 0)]


def shift(value, axis, k):
    return lax.ppermute(value, axis, [(i, (i + k) % 4) for i in range(4)])


def gather(value, axis):
    return [value] + [shift(value, axis, k) for k in (1, 2, 3)]


def scatter_term(pieces):
    got = [pieces[0]] + [shift(pieces[k], "y", k) for k in (1, 2, 3)]
    mine = ((got[0] + got[1]) + got[2]) + got[3]
    return mine, lax.ppermute(mine, "zh", SWAP)


def scatter_doc(own, other):
    got = lax.ppermute(other, "c", SWAP)
    pieces = [own[9 * k : 9 * k + 9] + got[9 * k : 9 * k + 9] for k in range(4)]
    got = [pieces[0]] + [shift(pieces[k], "x", k) for k in (1, 2, 3)]
    return gather(((got[0] + got[1]) + got[2]) + got[3], "zl")


def gather_doc(value):
    mine = gather(value, "x")
    return mine + [lax.ppermute(m, "c", SWAP) for m in mine]


def local(blocks, block_rows, block_cols, counts, start):
    docs = float(BR * BLK * 32)
    terms = float(BR * BLK * 8)
    index = (block_rows, block_cols, counts)

    *pieces, held, turned = call(
        first_forward,
        (*index, start, blocks),
        (panel(17),) * 4 + (TILE, TILE),
        [
            SMEM((1, NB), jnp.int32), SMEM((1, NB), jnp.int32), SMEM((1, 1), jnp.int32),
            SPLIT, held_panel(68),
            pltpu.SemaphoreType.DMA((NB // GROUP,)), pltpu.SemaphoreType.DMA((3,)),
        ],
        spaces=[ANY, ANY, ANY, VMEM, ANY],
        limit=30,
    )
    left_chunk, mr0 = call(left_first, scatter_term(pieces), (panel(17), SMALL), terms=terms)
    left1 = gather(left_chunk, "y")
    back_scratch = [SPLIT, held_panel(72), held_panel(4)]
    own, other = call(backward, (*index, *left1, held), (panel(36), panel(36)), back_scratch, limit=20)
    right_chunk, ml1, right0 = call(
        right_first, (*scatter_doc(own, other), start, mr0), (panel(9), SMALL, panel(8)),
        [VMEM((4, 9, K, BLK), F32)], docs=docs,
    )
    right1 = gather_doc(right_chunk)
    pieces = call(
        forward, (*index, *right1, turned), (panel(17),) * 4, [SPLIT, held_panel(68), held_panel(8)], limit=20
    )
    left2_chunk, mr1, h1 = call(
        left_second, (*scatter_term(pieces), left_chunk, ml1), (panel(17), SMALL, SMALL), terms=terms
    )
    left2 = gather(left2_chunk, "y")
    own, other = call(backward, (*index, *left2, held), (panel(36), panel(36)), back_scratch, limit=20)
    prior = call(right_prior, (*right1, start, mr0, mr1, h1), panel(BR))
    right2_chunk, ext, ml2, h2 = call(
        right_second, (*scatter_doc(own, other), right_chunk, right0, mr1, h1),
        (panel(8), SMALL, SMALL, SMALL),
        [VMEM((4, 9, K, BLK), F32), VMEM((8, 48, BLK), BF)], docs=docs,
    )
    right2 = gather_doc(right2_chunk)
    ext = ext + lax.ppermute(ext, "c", SWAP)
    ext = lax.all_to_all(jnp.broadcast_to(ext[None], (32, K, BLK)), ("x", "y", "zh"), 0, 0)
    left_out = call(left_result, (*left1, *left2, ml1, ml2, h2), WIDE)
    right_out = call(right_result, (ext, *right2, prior), WIDE, terms=terms)
    return left_out, right_out


def solution(mesh):
    fine = Mesh(np.asarray(mesh.devices).reshape(4, 4, 2, 4, 2), (*DOC, *TERM))
    return jax.shard_map(
        local,
        mesh=fine,
        in_specs=(P(DOC, TERM, None, None), P(DOC, TERM), P(DOC, TERM), P(DOC, TERM), P(None, TERM)),
        out_specs=(P(None, DOC), P(None, TERM)),
        check_vma=False,
    )
```

```python
import functools

import jax
import jax.numpy as jnp
import numpy as np
from jax import lax
from jax.experimental import pallas as pl
from jax.experimental.pallas import tpu as pltpu
from jax.sharding import Mesh
from jax.sharding import PartitionSpec as P

BLK = 128
K = 16
BR = 64
NB = 320
GROUP = 32
DOC = ("zl", "x", "c")
TERM = ("y", "zh")
F32 = jnp.float32
BF = jnp.bfloat16
HI = lax.Precision.HIGHEST
VMEM = pltpu.VMEM
SMEM = pltpu.SMEM
ANY = pl.ANY


def mm(a, b):
    return jnp.dot(a, b, precision=HI, preferred_element_type=F32)


def mmt(a, b):
    return lax.dot_general(a, b, (((1,), (1,)), ((), ())), precision=HI, preferred_element_type=F32)


def inverse_factor(gram):
    lane = lax.broadcasted_iota(jnp.int32, (K, BLK), 1)
    row = lax.broadcasted_iota(jnp.int32, (K, BLK), 0)
    left = columns(gram)
    result = jnp.where(lane == row, 1.0, 0.0)
    scale = jnp.zeros((K, BLK), F32)
    for j in range(K):
        pivot = left[j][j : j + 1, :]
        scale = jnp.where(row == j, lax.rsqrt(pivot), scale)
        if j == K - 1:
            break
        factor = jnp.where(row > j, left[j] * (1.0 / pivot), 0.0)
        result = result - factor * result[j : j + 1, :]
        for k in range(j + 1, K):
            left[k] = left[k] - factor * left[k][j : j + 1, :]
    return (result * scale)[:, 0:K]


def projected(ext, count):
    proj = ext[:, K : 2 * K] / count
    return proj, inverse_factor(ext[:, 0:K] / count - mmt(proj, proj))


def columns(matrix):
    return [jnp.broadcast_to(matrix[:, j : j + 1], (K, BLK)) for j in range(K)]


def combine(cols, piece):
    total = cols[0] * piece[0:1, :]
    for j in range(1, K):
        total = total + cols[j] * piece[j : j + 1, :]
    return total


def parts(value):
    high = value.astype(BF)
    rest = value - high.astype(F32)
    middle = rest.astype(BF)
    low = (rest - middle.astype(F32)).astype(BF)
    return high, middle, low


def stacked(value):
    return jnp.concatenate(parts(value), axis=0)


def split_store(split_ref, index, value):
    high, middle, low = parts(value)
    split_ref[index, 0:16, :] = high
    split_ref[index, 16:32, :] = middle
    split_ref[index, 32:48, :] = low


def each(count, body, unroll=4):
    def step(i, carry):
        body(i)
        return carry

    lax.fori_loop(0, count, step, 0, unroll=unroll)


def split_all(split_ref, base, piece, count):
    each(count, lambda i: split_store(split_ref, base + i, piece[i]), 8)


def cross(left, right):
    return lax.dot_general(left, right, (((1,), (1,)), ((), ())), preferred_element_type=F32)


def fold(wide):
    rows = (wide[32:48, :] + wide[16:32, :]) + wide[0:16, :]
    return (rows[:, 32:48] + rows[:, 16:32]) + rows[:, 0:16]


def pad_lanes(*pieces):
    width = sum(p.shape[1] for p in pieces)
    return jnp.concatenate([*pieces, jnp.zeros((K, BLK - width), F32)], axis=1)


def spin(index, step):
    return jnp.bitwise_and(index - step, 3)


def group_of(base, live, src_ref, tgt_ref, block, split, acc, place, spare):
    spots, values = [], []
    for u in range(GROUP):
        slot = base + u
        wide = jnp.dot(split[src_ref[0, slot]], block(slot), preferred_element_type=F32)
        values.append((wide[32:48, :] + wide[16:32, :]) + wide[0:16, :])
        spots.append(jnp.where(slot < live, place(tgt_ref[0, slot]), spare))
    for spot, value in zip(spots, values):
        acc[spot] += value


def term_place(y):
    def place(target):
        part = jnp.bitwise_and(lax.shift_right_logical(target, 4) - y, 3)
        return part * 17 + jnp.bitwise_and(target, 15)

    return place


def doc_place(x, core):
    def place(target):
        half = jnp.bitwise_xor(lax.shift_right_logical(target, 5), core)
        part = jnp.bitwise_and(lax.shift_right_logical(target, 3) - x, 3)
        return half * 36 + part * 9 + jnp.bitwise_and(target, 7)

    return place


def multiply(live, src_ref, tgt_ref, held, split, acc, place, spare):
    def step(g, carry):
        group_of(g * GROUP, live, src_ref, tgt_ref, lambda s: held[s], split, acc, place, spare)
        return carry

    lax.fori_loop(0, lax.div(live + (GROUP - 1), GROUP), step, 0)


def gram_step(count, value_of, total, unroll=8):
    def step(i, carry):
        value = value_of(i)
        return carry + cross(value, value)

    return lax.fori_loop(0, count, step, total, unroll=unroll)


def first_forward(
    rows_any, cols_any, counts_any, start_any, blocks, o0, o1, o2, o3, held, turned,
    rows, cols, counts, start, split, acc, sems, small_sems,
):
    groups = NB // GROUP
    small = [
        pltpu.make_async_copy(start_any, start, small_sems.at[0]),
        pltpu.make_async_copy(rows_any, rows, small_sems.at[1]),
        pltpu.make_async_copy(cols_any, cols, small_sems.at[2]),
        pltpu.make_async_copy(counts_any, counts, small_sems.at[3]),
    ]
    for copy in small:
        copy.start()
    for i in range(groups):
        part = pl.ds(i * GROUP, GROUP)
        pltpu.make_async_copy(blocks.at[0, part], held.at[part], sems.at[i]).start()
    acc[...] = jnp.zeros_like(acc)
    for copy in small:
        copy.wait()

    def prepare(i):
        value = stacked(start[:, pl.ds(pl.multiple_of(i * BLK, BLK), BLK)])
        split[i] = value
        return value

    ext = pad_lanes(fold(gram_step(BR, prepare, jnp.zeros((48, 48), F32), 16)))
    live = counts[0, 0]
    place = term_place(lax.axis_index("y"))

    def turn(slot):
        value = held[slot].T
        turned[slot] = value
        return value

    def step(i, carry):
        part = pl.ds(i * GROUP, GROUP)
        pltpu.make_async_copy(blocks.at[0, part], held.at[part], sems.at[i]).wait()

        @pl.when(i * GROUP < live)
        def _():
            group_of(i * GROUP, live, cols, rows, turn, split, acc, place, 16)

        return carry

    lax.fori_loop(0, groups, step, 0)
    for k, out in enumerate((o0, o1, o2, o3)):
        out[0:16] = acc[k * 17 : k * 17 + 16]
        out[16] = ext


def forward(rows, cols, counts, r0, r1, r2, r3, w0, w1, w2, w3, turned, o0, o1, o2, o3, split, acc, grams):
    x, core = lax.axis_index("x"), lax.axis_index("c")
    acc[...] = jnp.zeros_like(acc)
    for side, pieces in ((core, (r0, r1, r2, r3)), (1 - core, (w0, w1, w2, w3))):
        for k, piece in enumerate(pieces):
            base = side * 32 + spin(x, k) * 8
            split_all(split, base, piece, 8)
            grams[side * 4 + spin(x, k)] = piece[8]
    multiply(counts[0, 0], cols, rows, turned, split, acc, term_place(lax.axis_index("y")), 16)
    ext = grams[0]
    for i in range(1, 8):
        ext = ext + grams[i]
    for k, out in enumerate((o0, o1, o2, o3)):
        out[0:16] = acc[k * 17 : k * 17 + 16]
        out[16] = ext


def backward(rows, cols, counts, p0, p1, p2, p3, held, own, other, split, acc, grams):
    y = lax.axis_index("y")
    acc[...] = jnp.zeros_like(acc)
    for k, piece in enumerate((p0, p1, p2, p3)):
        base = spin(y, k) * 16
        split_all(split, base, piece, 16)
        grams[spin(y, k)] = piece[16]
    place = doc_place(lax.axis_index("x"), lax.axis_index("c"))
    multiply(counts[0, 0], rows, cols, held, split, acc, place, 8)
    ext = ((grams[0] + grams[1]) + grams[2]) + grams[3]
    for j in range(8):
        acc[j * 9 + 8] = ext
    own[...] = acc[0:36]
    other[...] = acc[36:72]


def left_first(mine, theirs, out, mr0, *, terms):
    inverse = inverse_factor((mine[16] + theirs[16])[:, 0:K] / terms)
    mr0[...] = pad_lanes(inverse)
    cols = columns(inverse)
    gram = jnp.zeros((48, 48), F32)
    for i in range(16):
        value = combine(cols, mine[i] + theirs[i])
        out[i] = value
        wide = stacked(value)
        gram = gram + cross(wide, wide)
    out[16] = pad_lanes(fold(gram))


def zl_total(t0, t1, t2, t3, order):
    zl = lax.axis_index("zl")
    for k, piece in enumerate((t0, t1, t2, t3)):
        order[spin(zl, k)] = piece[...]
    return lambda i: ((order[0, i] + order[1, i]) + order[2, i]) + order[3, i]


def right_first(t0, t1, t2, t3, start, mr0, out, ml1, right0, order, *, docs):
    total = zl_total(t0, t1, t2, t3, order)
    x, core = lax.axis_index("x"), lax.axis_index("c")
    first = (core * 32 + x * 8) * BLK
    inverse = inverse_factor(total(8)[:, 0:K] / docs)
    ml1[...] = pad_lanes(inverse)
    cols_0 = columns(mr0[:, 0:K])
    cols_1 = columns(inverse)
    gram = jnp.zeros((48, 48), F32)
    mixed = jnp.zeros((48, 48), F32)
    for i in range(8):
        source = pl.ds(pl.multiple_of(first + i * BLK, BLK), BLK)
        prior = combine(cols_0, start[:, source])
        right0[i] = prior
        value = combine(cols_1, total(i))
        out[i] = value
        wide = stacked(value)
        gram = gram + cross(wide, wide)
        mixed = mixed + cross(wide, stacked(prior))
    out[8] = pad_lanes(fold(gram), fold(mixed))


def left_second(mine, theirs, left_raw, ml1, out, mr1, h1, *, terms):
    proj, inverse = projected(mine[16] + theirs[16], terms)
    mr1[...] = pad_lanes(inverse)
    h1[...] = pad_lanes(proj)
    cols_l = columns(ml1[:, 0:K])
    cols_h = columns(proj)
    for i in range(16):
        out[i] = (mine[i] + theirs[i]) - combine(cols_h, left_raw[i])
    cols_m = columns(inverse)
    gram = jnp.zeros((48, 48), F32)
    mixed = jnp.zeros((48, 48), F32)
    for i in range(16):
        prior = stacked(combine(cols_l, left_raw[i]))
        value = combine(cols_m, out[i])
        out[i] = value
        wide = stacked(value)
        gram = gram + cross(wide, wide)
        mixed = mixed + cross(wide, prior)
    out[16] = pad_lanes(fold(gram), fold(mixed))


def right_second(t0, t1, t2, t3, right_raw, prior, out, ext_out, ml2, h2, order, *, docs):
    total = zl_total(t0, t1, t2, t3, order)
    first = lax.axis_index("c") * 32 + lax.axis_index("x") * 8
    proj, inverse = projected(total(8), docs)
    ml2[...] = pad_lanes(inverse)
    h2[...] = pad_lanes(proj)
    cols_h = columns(proj)
    for i in range(8):
        out[i] = total(i) - combine(cols_h, right_raw[i])
    cols_m = columns(inverse)
    gram = jnp.zeros((48, 48), F32)
    mixed = jnp.zeros((48, 48), F32)
    for i in range(8):
        value = combine(cols_m, out[i])
        out[i] = value
        wide = stacked(value)
        gram = gram + cross(wide, wide)
        mixed = mixed + cross(wide, stacked(prior[first + i]))
    ext_out[...] = pad_lanes(fold(gram), fold(mixed))


def lanes(index):
    return pl.ds(pl.multiple_of(index * BLK, BLK), BLK)


def left_result(a0, a1, a2, a3, b0, b1, b2, b3, ml1, ml2, h2, out):
    y = lax.axis_index("y")
    cols_1 = columns(ml1[:, 0:K])
    for k, first in enumerate((a0, a1, a2, a3)):
        base = spin(y, k) * 16

        def prior(i, base=base, first=first):
            out[:, lanes(base + i)] = combine(cols_1, first[i])

        each(16, prior)
    cols_h = columns(h2[:, 0:K])
    for k, second in enumerate((b0, b1, b2, b3)):
        base = spin(y, k) * 16

        def rest(i, base=base, second=second):
            part = lanes(base + i)
            out[:, part] = second[i] - combine(cols_h, out[:, part])

        each(16, rest)
    cols_2 = columns(ml2[:, 0:K])

    def final(i):
        out[:, lanes(i)] = combine(cols_2, out[:, lanes(i)])

    each(BR, final)


def by_side(pieces):
    x, core = lax.axis_index("x"), lax.axis_index("c")
    for n, piece in enumerate(pieces):
        side = core if n < 4 else 1 - core
        yield side * 32 + spin(x, n % 4) * 8, piece


def right_prior(r0, r1, r2, r3, w0, w1, w2, w3, start, mr0, mr1, h1, out):
    cols_0 = columns(mr0[:, 0:K])

    def from_start(i):
        out[i] = combine(cols_0, start[:, lanes(i)])

    each(BR, from_start)
    cols_h = columns(h1[:, 0:K])
    for base, piece in by_side((r0, r1, r2, r3, w0, w1, w2, w3)):

        def rest(i, base=base, piece=piece):
            out[base + i] = piece[i] - combine(cols_h, out[base + i])

        each(8, rest)
    cols_1 = columns(mr1[:, 0:K])

    def final(i):
        out[i] = combine(cols_1, out[i])

    each(BR, final)


def right_result(ext_a, ext_b, r0, r1, r2, r3, w0, w1, w2, w3, right1, out, *, terms):
    proj, inverse = projected(ext_a[...] + ext_b[...], terms)
    cols_h = columns(proj)
    for base, piece in by_side((r0, r1, r2, r3, w0, w1, w2, w3)):

        def rest(i, base=base, piece=piece):
            out[:, lanes(base + i)] = piece[i] - combine(cols_h, right1[base + i])

        each(8, rest)
    cols_m = columns(inverse)

    def final(i):
        out[:, lanes(i)] = combine(cols_m, out[:, lanes(i)])

    each(BR, final)


def panel(n):
    return jax.ShapeDtypeStruct((n, K, BLK), F32)


SMALL = jax.ShapeDtypeStruct((K, BLK), F32)
WIDE = jax.ShapeDtypeStruct((K, BR * BLK), F32)
TILE = jax.ShapeDtypeStruct((NB, BLK, BLK), BF)
SPLIT = VMEM((BR, 48, BLK), BF)


def held_panel(n):
    return VMEM((n, K, BLK), F32)


def call(body, args, outs, scratch=(), spaces=None, limit=8, micros=2, **constants):
    def space(a):
        return SMEM if a.dtype == jnp.int32 else VMEM

    spaces = spaces or [space(a) for a in args]
    return pl.pallas_call(
        functools.partial(body, **constants) if constants else body,
        name=body.__name__,
        out_shape=outs,
        in_specs=[pl.BlockSpec(memory_space=s) for s in spaces],
        out_specs=jax.tree.map(lambda _: pl.BlockSpec(memory_space=VMEM), outs),
        scratch_shapes=list(scratch),
        cost_estimate=pl.CostEstimate(
            flops=micros * 1000000000, bytes_accessed=micros * 1000000, transcendentals=0
        ),
        compiler_params=pltpu.CompilerParams(vmem_limit_bytes=limit * 1024 * 1024),
    )(*args)


SWAP = [(0, 1), (1, 0)]


def shift(value, axis, k):
    return lax.ppermute(value, axis, [(i, (i + k) % 4) for i in range(4)])


def gather(value, axis):
    return [value] + [shift(value, axis, k) for k in (1, 2, 3)]


def total_of(got):
    return ((got[0] + got[1]) + got[2]) + got[3]


def in_order(got):
    stack = jnp.stack(got)
    x = lax.axis_index("x")
    return total_of([lax.dynamic_index_in_dim(stack, spin(x, k), 0, False) for k in range(4)])


def scatter_term(pieces):
    got = [pieces[0]] + [shift(pieces[k], "y", k) for k in (1, 2, 3)]
    mine = total_of(got)
    return mine, lax.ppermute(mine, "zh", SWAP)


def scatter_doc(own, other):
    got = lax.ppermute(other, "c", SWAP)
    pieces = [own[9 * k : 9 * k + 9] + got[9 * k : 9 * k + 9] for k in range(4)]
    got = [pieces[0]] + [shift(pieces[k], "x", k) for k in (1, 2, 3)]
    return gather(total_of(got), "zl")


def gather_doc(value):
    mine = gather(value, "x")
    return mine + [lax.ppermute(m, "c", SWAP) for m in mine]


def local(blocks, block_rows, block_cols, counts, start):
    docs = float(BR * BLK * 32)
    terms = float(BR * BLK * 8)
    index = (block_rows, block_cols, counts)

    *pieces, held, turned = call(
        first_forward,
        (*index, start, blocks),
        (panel(17),) * 4 + (TILE, TILE),
        [
            SMEM((1, NB), jnp.int32), SMEM((1, NB), jnp.int32), SMEM((1, 1), jnp.int32),
            VMEM((K, BR * BLK), F32), SPLIT, held_panel(68),
            pltpu.SemaphoreType.DMA((NB // GROUP,)), pltpu.SemaphoreType.DMA((4,)),
        ],
        spaces=[pltpu.HBM] * 5,
        limit=30,
    )
    left_chunk, mr0 = call(left_first, scatter_term(pieces), (panel(17), SMALL), terms=terms)
    left1 = gather(left_chunk, "y")
    back_scratch = [SPLIT, held_panel(72), held_panel(4)]
    own, other = call(backward, (*index, *left1, held), (panel(36), panel(36)), back_scratch, limit=20)
    right_chunk, ml1, right0 = call(
        right_first, (*scatter_doc(own, other), start, mr0), (panel(9), SMALL, panel(8)),
        [VMEM((4, 9, K, BLK), F32)], docs=docs,
    )
    right1 = gather_doc(right_chunk)
    pieces = call(
        forward, (*index, *right1, turned), (panel(17),) * 4, [SPLIT, held_panel(68), held_panel(8)], limit=20
    )
    left2_chunk, mr1, h1 = call(
        left_second, (*scatter_term(pieces), left_chunk, ml1), (panel(17), SMALL, SMALL), terms=terms
    )
    left2 = gather(left2_chunk, "y")
    own, other = call(backward, (*index, *left2, held), (panel(36), panel(36)), back_scratch, limit=20)
    prior = call(right_prior, (*right1, start, mr0, mr1, h1), panel(BR))
    right2_chunk, ext, ml2, h2 = call(
        right_second, (*scatter_doc(own, other), right_chunk, prior),
        (panel(8), SMALL, SMALL, SMALL), [VMEM((4, 9, K, BLK), F32)], docs=docs,
    )
    ext = ext + lax.ppermute(ext, "zh", SWAP)
    mine = gather(right2_chunk, "x")
    left_out = call(left_result, (*left1, *left2, ml1, ml2, h2), WIDE)
    ext, left_out, *mine = lax.optimization_barrier((ext, left_out, *mine))
    ext = total_of(gather(ext, "y"))
    right2 = mine + [lax.ppermute(m, "c", SWAP) for m in mine]
    ext = in_order(gather(ext, "x"))
    right_out = call(
        right_result, (ext, lax.ppermute(ext, "c", SWAP), *right2, prior), WIDE, terms=terms
    )
    return left_out, right_out


def solution(mesh):
    fine = Mesh(np.asarray(mesh.devices).reshape(4, 4, 2, 4, 2), (*DOC, *TERM))
    return jax.shard_map(
        local,
        mesh=fine,
        in_specs=(P(DOC, TERM, None, None), P(DOC, TERM), P(DOC, TERM), P(DOC, TERM), P(None, TERM)),
        out_specs=(P(None, DOC), P(None, TERM)),
        check_vma=False,
    )
```

```python
import functools

import jax
import jax.numpy as jnp
import numpy as np
from jax import lax
from jax.experimental import pallas as pl
from jax.experimental.pallas import tpu as pltpu
from jax.sharding import Mesh
from jax.sharding import PartitionSpec as P

BLK = 128
K = 16
BR = 64
NB = 320
GROUP = 32
SHARERS = 64
DOC = ("zl", "x", "c")
TERM = ("y", "zh")
F32 = jnp.float32
BF = jnp.bfloat16
HI = lax.Precision.HIGHEST
VMEM = pltpu.VMEM
SMEM = pltpu.SMEM
ANY = pl.ANY


def mm(a, b):
    return jnp.dot(a, b, precision=HI, preferred_element_type=F32)


def mmt(a, b):
    return lax.dot_general(a, b, (((1,), (1,)), ((), ())), precision=HI, preferred_element_type=F32)


def inverse_factor(gram):
    lane = lax.broadcasted_iota(jnp.int32, (K, BLK), 1)
    row = lax.broadcasted_iota(jnp.int32, (K, BLK), 0)
    left = columns(gram)
    result = jnp.where(lane == row, 1.0, 0.0)
    scale = jnp.zeros((K, BLK), F32)
    for j in range(K):
        pivot = left[j][j : j + 1, :]
        scale = jnp.where(row == j, lax.rsqrt(pivot), scale)
        if j == K - 1:
            break
        factor = jnp.where(row > j, left[j] * (1.0 / pivot), 0.0)
        result = result - factor * result[j : j + 1, :]
        for k in range(j + 1, K):
            left[k] = left[k] - factor * left[k][j : j + 1, :]
    return (result * scale)[:, 0:K]


def projected(ext, count):
    proj = ext[:, K : 2 * K] / count
    return proj, inverse_factor(ext[:, 0:K] / count - mmt(proj, proj))


def columns(matrix):
    return [jnp.broadcast_to(matrix[:, j : j + 1], (K, BLK)) for j in range(K)]


def combine(cols, piece):
    total = cols[0] * piece[0:1, :]
    for j in range(1, K):
        total = total + cols[j] * piece[j : j + 1, :]
    return total


def parts(value):
    high = value.astype(BF)
    rest = value - high.astype(F32)
    middle = rest.astype(BF)
    low = (rest - middle.astype(F32)).astype(BF)
    return high, middle, low


def stacked(value):
    return jnp.concatenate(parts(value), axis=0)


def split_store(split_ref, index, value):
    high, middle, low = parts(value)
    split_ref[index, 0:16, :] = high
    split_ref[index, 16:32, :] = middle
    split_ref[index, 32:48, :] = low


def each(count, body, unroll=4):
    def step(i, carry):
        body(i)
        return carry

    lax.fori_loop(0, count, step, 0, unroll=unroll)


def split_all(split_ref, base, piece, count):
    each(count, lambda i: split_store(split_ref, base + i, piece[i]), 8)


def cross(left, right):
    return lax.dot_general(left, right, (((1,), (1,)), ((), ())), preferred_element_type=F32)


def fold(wide):
    rows = (wide[32:48, :] + wide[16:32, :]) + wide[0:16, :]
    return (rows[:, 32:48] + rows[:, 16:32]) + rows[:, 0:16]


def pad_lanes(*pieces):
    width = sum(p.shape[1] for p in pieces)
    return jnp.concatenate([*pieces, jnp.zeros((K, BLK - width), F32)], axis=1)


def spin(index, step):
    return jnp.bitwise_and(index - step, 3)


def group_of(base, live, src_ref, tgt_ref, block, split, acc, place, spare):
    spots, values = [], []
    for u in range(GROUP):
        slot = base + u
        wide = jnp.dot(split[src_ref[0, slot]], block(slot), preferred_element_type=F32)
        values.append((wide[32:48, :] + wide[16:32, :]) + wide[0:16, :])
        spots.append(jnp.where(slot < live, place(tgt_ref[0, slot]), spare))
    for spot, value in zip(spots, values):
        acc[spot] += value


def term_place(y):
    def place(target):
        part = jnp.bitwise_and(lax.shift_right_logical(target, 4) - y, 3)
        return part * 17 + jnp.bitwise_and(target, 15)

    return place


def doc_place(x, core):
    def place(target):
        half = jnp.bitwise_xor(lax.shift_right_logical(target, 5), core)
        part = jnp.bitwise_and(lax.shift_right_logical(target, 3) - x, 3)
        return half * 36 + part * 9 + jnp.bitwise_and(target, 7)

    return place


def multiply(live, src_ref, tgt_ref, held, split, acc, place, spare):
    def step(g, carry):
        group_of(g * GROUP, live, src_ref, tgt_ref, lambda s: held[s], split, acc, place, spare)
        return carry

    lax.fori_loop(0, lax.div(live + (GROUP - 1), GROUP), step, 0)


def gram_step(count, value_of, total, unroll=8):
    def step(i, carry):
        value = value_of(i)
        return carry + cross(value, value)

    return lax.fori_loop(0, count, step, total, unroll=unroll)


def first_forward(
    rows_any, cols_any, counts_any, start_any, blocks, o0, o1, o2, o3, held, turned,
    rows, cols, counts, start, split, acc, sems, small_sems,
):
    groups = NB // GROUP
    small = [
        pltpu.make_async_copy(start_any, start, small_sems.at[0]),
        pltpu.make_async_copy(rows_any, rows, small_sems.at[1]),
        pltpu.make_async_copy(cols_any, cols, small_sems.at[2]),
        pltpu.make_async_copy(counts_any, counts, small_sems.at[3]),
    ]
    for copy in small:
        copy.start()
    for i in range(groups):
        part = pl.ds(i * GROUP, GROUP)
        pltpu.make_async_copy(blocks.at[0, part], held.at[part], sems.at[i]).start()
    acc[...] = jnp.zeros_like(acc)
    for copy in small:
        copy.wait()

    def prepare(i):
        value = stacked(start[:, pl.ds(pl.multiple_of(i * BLK, BLK), BLK)])
        split[i] = value
        return value

    ext = pad_lanes(fold(gram_step(BR, prepare, jnp.zeros((48, 48), F32), 16)))
    live = counts[0, 0]
    place = term_place(lax.axis_index("y"))

    def turn(slot):
        value = held[slot].T
        turned[slot] = value
        return value

    def step(i, carry):
        part = pl.ds(i * GROUP, GROUP)
        pltpu.make_async_copy(blocks.at[0, part], held.at[part], sems.at[i]).wait()

        @pl.when(i * GROUP < live)
        def _():
            group_of(i * GROUP, live, cols, rows, turn, split, acc, place, 16)

        return carry

    lax.fori_loop(0, groups, step, 0)
    for k, out in enumerate((o0, o1, o2, o3)):
        out[0:16] = acc[k * 17 : k * 17 + 16]
        out[16] = ext


def forward(rows, cols, counts, r0, r1, r2, r3, w0, w1, w2, w3, turned, o0, o1, o2, o3, split, acc, grams):
    x, core = lax.axis_index("x"), lax.axis_index("c")
    acc[...] = jnp.zeros_like(acc)
    for side, pieces in ((core, (r0, r1, r2, r3)), (1 - core, (w0, w1, w2, w3))):
        for k, piece in enumerate(pieces):
            base = side * 32 + spin(x, k) * 8
            split_all(split, base, piece, 8)
            grams[side * 4 + spin(x, k)] = piece[8]
    multiply(counts[0, 0], cols, rows, turned, split, acc, term_place(lax.axis_index("y")), 16)
    ext = grams[0]
    for i in range(1, 8):
        ext = ext + grams[i]
    for k, out in enumerate((o0, o1, o2, o3)):
        out[0:16] = acc[k * 17 : k * 17 + 16]
        out[16] = ext


def backward(rows, cols, counts, p0, p1, p2, p3, held, own, other, split, acc, grams):
    y = lax.axis_index("y")
    acc[...] = jnp.zeros_like(acc)
    for k, piece in enumerate((p0, p1, p2, p3)):
        base = spin(y, k) * 16
        split_all(split, base, piece, 16)
        grams[spin(y, k)] = piece[16]
    place = doc_place(lax.axis_index("x"), lax.axis_index("c"))
    multiply(counts[0, 0], rows, cols, held, split, acc, place, 8)
    ext = ((grams[0] + grams[1]) + grams[2]) + grams[3]
    for j in range(8):
        acc[j * 9 + 8] = ext
    own[...] = acc[0:36]
    other[...] = acc[36:72]


def left_first(mine, theirs, out, mr0, *, terms):
    inverse = inverse_factor((mine[16] + theirs[16])[:, 0:K] / terms)
    mr0[...] = pad_lanes(inverse)
    cols = columns(inverse)
    gram = jnp.zeros((48, 48), F32)
    for i in range(16):
        value = combine(cols, mine[i] + theirs[i])
        out[i] = value
        wide = stacked(value)
        gram = gram + cross(wide, wide)
    out[16] = pad_lanes(fold(gram))


def zl_total(t0, t1, t2, t3, order):
    zl = lax.axis_index("zl")
    for k, piece in enumerate((t0, t1, t2, t3)):
        order[spin(zl, k)] = piece[...]
    return lambda i: ((order[0, i] + order[1, i]) + order[2, i]) + order[3, i]


def right_first(t0, t1, t2, t3, start, mr0, out, ml1, right0, order, *, docs):
    total = zl_total(t0, t1, t2, t3, order)
    x, core = lax.axis_index("x"), lax.axis_index("c")
    first = (core * 32 + x * 8) * BLK
    inverse = inverse_factor(total(8)[:, 0:K] / docs)
    ml1[...] = pad_lanes(inverse)
    cols_0 = columns(mr0[:, 0:K])
    cols_1 = columns(inverse)
    gram = jnp.zeros((48, 48), F32)
    mixed = jnp.zeros((48, 48), F32)
    for i in range(8):
        source = pl.ds(pl.multiple_of(first + i * BLK, BLK), BLK)
        prior = combine(cols_0, start[:, source])
        right0[i] = prior
        value = combine(cols_1, total(i))
        out[i] = value
        wide = stacked(value)
        gram = gram + cross(wide, wide)
        mixed = mixed + cross(wide, stacked(prior))
    out[8] = pad_lanes(fold(gram), fold(mixed))


def left_second(mine, theirs, left_raw, ml1, out, mr1, h1, *, terms):
    proj, inverse = projected(mine[16] + theirs[16], terms)
    mr1[...] = pad_lanes(inverse)
    h1[...] = pad_lanes(proj)
    cols_l = columns(ml1[:, 0:K])
    cols_h = columns(proj)
    for i in range(16):
        out[i] = (mine[i] + theirs[i]) - combine(cols_h, left_raw[i])
    cols_m = columns(inverse)
    gram = jnp.zeros((48, 48), F32)
    mixed = jnp.zeros((48, 48), F32)
    for i in range(16):
        prior = stacked(combine(cols_l, left_raw[i]))
        value = combine(cols_m, out[i])
        out[i] = value
        wide = stacked(value)
        gram = gram + cross(wide, wide)
        mixed = mixed + cross(wide, prior)
    out[16] = pad_lanes(fold(gram), fold(mixed))


def right_second(t0, t1, t2, t3, right_raw, prior, out, ext_out, ml2, h2, order, *, docs):
    total = zl_total(t0, t1, t2, t3, order)
    first = lax.axis_index("c") * 32 + lax.axis_index("x") * 8
    proj, inverse = projected(total(8), docs)
    ml2[...] = pad_lanes(inverse)
    h2[...] = pad_lanes(proj)
    cols_h = columns(proj)
    for i in range(8):
        out[i] = total(i) - combine(cols_h, right_raw[i])
    cols_m = columns(inverse)
    gram = jnp.zeros((48, 48), F32)
    mixed = jnp.zeros((48, 48), F32)
    for i in range(8):
        value = combine(cols_m, out[i])
        out[i] = value
        wide = stacked(value)
        gram = gram + cross(wide, wide)
        mixed = mixed + cross(wide, prior[first + i])
    both = jnp.concatenate([fold(gram), fold(mixed)], axis=1)
    ext_out[...] = jnp.broadcast_to(
        jnp.concatenate([both[0:8], both[8:16], jnp.zeros((8, 64), F32)], axis=1)[None], (SHARERS, 8, BLK)
    )


def lanes(index):
    return pl.ds(pl.multiple_of(index * BLK, BLK), BLK)


def factor_parts(*matrices):
    tall = [jnp.concatenate([p.astype(F32) for p in parts(m)], axis=0) for m in matrices]
    return jnp.concatenate([t for t in tall for _ in range(3)], axis=1).astype(BF)


def mix(factors, first, second):
    wide = jnp.dot(factors, jnp.concatenate([first, second], axis=0), preferred_element_type=F32)
    return (wide[32:48, :] + wide[16:32, :]) + wide[0:16, :]


def left_result(a0, a1, a2, a3, b0, b1, b2, b3, ml1, ml2, h2, out):
    y = lax.axis_index("y")
    inverse = ml2[:, 0:K]
    factors = factor_parts(inverse, -mm(mm(inverse, h2[:, 0:K]), ml1[:, 0:K]))
    for k, (first, second) in enumerate(zip((a0, a1, a2, a3), (b0, b1, b2, b3))):
        base = spin(y, k) * 16

        def result(i, base=base, first=first, second=second):
            out[:, lanes(base + i)] = mix(factors, stacked(second[i]), stacked(first[i]))

        each(16, result, 8)


def by_side(pieces):
    x, core = lax.axis_index("x"), lax.axis_index("c")
    for n, piece in enumerate(pieces):
        side = core if n < 4 else 1 - core
        yield side * 32 + spin(x, n % 4) * 8, piece


def right_prior(r0, r1, r2, r3, w0, w1, w2, w3, start, mr0, mr1, h1, out, work):
    cols_0 = columns(mr0[:, 0:K])

    def from_start(i):
        work[i] = combine(cols_0, start[:, lanes(i)])

    each(BR, from_start)
    cols_h = columns(h1[:, 0:K])
    for base, piece in by_side((r0, r1, r2, r3, w0, w1, w2, w3)):

        def rest(i, base=base, piece=piece):
            work[base + i] = piece[i] - combine(cols_h, work[base + i])

        each(8, rest)
    cols_1 = columns(mr1[:, 0:K])

    def final(i):
        split_store(out, i, combine(cols_1, work[i]))

    each(BR, final)


def right_result(ext, r0, r1, r2, r3, w0, w1, w2, w3, right1, out, *, terms):
    total = ext[0]
    for i in range(1, SHARERS):
        total = total + ext[i]
    both = jnp.concatenate([total[:, 0 : 2 * K], total[:, 2 * K : 4 * K]], axis=0)
    proj, inverse = projected(both, terms)
    factors = factor_parts(inverse, -mm(inverse, proj))
    for base, piece in by_side((r0, r1, r2, r3, w0, w1, w2, w3)):

        def result(i, base=base, piece=piece):
            out[:, lanes(base + i)] = mix(factors, stacked(piece[i]), right1[base + i])

        each(8, result, 8)


def panel(n):
    return jax.ShapeDtypeStruct((n, K, BLK), F32)


SMALL = jax.ShapeDtypeStruct((K, BLK), F32)
WIDE = jax.ShapeDtypeStruct((K, BR * BLK), F32)
TILE = jax.ShapeDtypeStruct((NB, BLK, BLK), BF)
SPLIT = VMEM((BR, 48, BLK), BF)


def held_panel(n):
    return VMEM((n, K, BLK), F32)


def call(body, args, outs, scratch=(), spaces=None, limit=8, micros=2, **constants):
    def space(a):
        return SMEM if a.dtype == jnp.int32 else VMEM

    spaces = spaces or [space(a) for a in args]
    return pl.pallas_call(
        functools.partial(body, **constants) if constants else body,
        name=body.__name__,
        out_shape=outs,
        in_specs=[pl.BlockSpec(memory_space=s) for s in spaces],
        out_specs=jax.tree.map(lambda _: pl.BlockSpec(memory_space=VMEM), outs),
        scratch_shapes=list(scratch),
        cost_estimate=pl.CostEstimate(
            flops=micros * 1000000000, bytes_accessed=micros * 1000000, transcendentals=0
        ),
        compiler_params=pltpu.CompilerParams(vmem_limit_bytes=limit * 1024 * 1024),
    )(*args)


SWAP = [(0, 1), (1, 0)]


def shift(value, axis, k):
    return lax.ppermute(value, axis, [(i, (i + k) % 4) for i in range(4)])


def gather(value, axis):
    return [value] + [shift(value, axis, k) for k in (1, 2, 3)]


def total_of(got):
    return ((got[0] + got[1]) + got[2]) + got[3]


def scatter_term(pieces):
    got = [pieces[0]] + [shift(pieces[k], "y", k) for k in (1, 2, 3)]
    mine = total_of(got)
    return mine, lax.ppermute(mine, "zh", SWAP)


def scatter_doc(own, other):
    got = lax.ppermute(other, "c", SWAP)
    pieces = [own[9 * k : 9 * k + 9] + got[9 * k : 9 * k + 9] for k in range(4)]
    got = [pieces[0]] + [shift(pieces[k], "x", k) for k in (1, 2, 3)]
    return gather(total_of(got), "zl")


def gather_doc(value):
    mine = gather(value, "x")
    return mine + [lax.ppermute(m, "c", SWAP) for m in mine]


def local(blocks, block_rows, block_cols, counts, start):
    docs = float(BR * BLK * 32)
    terms = float(BR * BLK * 8)
    index = (block_rows, block_cols, counts)

    *pieces, held, turned = call(
        first_forward,
        (*index, start, blocks),
        (panel(17),) * 4 + (TILE, TILE),
        [
            SMEM((1, NB), jnp.int32), SMEM((1, NB), jnp.int32), SMEM((1, 1), jnp.int32),
            VMEM((K, BR * BLK), F32), SPLIT, held_panel(68),
            pltpu.SemaphoreType.DMA((NB // GROUP,)), pltpu.SemaphoreType.DMA((4,)),
        ],
        spaces=[pltpu.HBM] * 5,
        limit=30,
    )
    left_chunk, mr0 = call(left_first, scatter_term(pieces), (panel(17), SMALL), terms=terms)
    left1 = gather(left_chunk, "y")
    back_scratch = [SPLIT, held_panel(72), held_panel(4)]
    own, other = call(backward, (*index, *left1, held), (panel(36), panel(36)), back_scratch, limit=20)
    right_chunk, ml1, right0 = call(
        right_first, (*scatter_doc(own, other), start, mr0), (panel(9), SMALL, panel(8)),
        [VMEM((4, 9, K, BLK), F32)], docs=docs,
    )
    right1 = gather_doc(right_chunk)
    pieces = call(
        forward, (*index, *right1, turned), (panel(17),) * 4, [SPLIT, held_panel(68), held_panel(8)], limit=20
    )
    left2_chunk, mr1, h1 = call(
        left_second, (*scatter_term(pieces), left_chunk, ml1), (panel(17), SMALL, SMALL), terms=terms
    )
    left2 = gather(left2_chunk, "y")
    own, other = call(backward, (*index, *left2, held), (panel(36), panel(36)), back_scratch, limit=20)
    prior = call(
        right_prior, (*right1, start, mr0, mr1, h1), jax.ShapeDtypeStruct((BR, 48, BLK), BF), [held_panel(BR)]
    )
    right2_chunk, ext, ml2, h2 = call(
        right_second, (*scatter_doc(own, other), right_chunk, prior),
        (panel(8), jax.ShapeDtypeStruct((SHARERS, 8, BLK), F32), SMALL, SMALL),
        [VMEM((4, 9, K, BLK), F32)], docs=docs,
    )
    mine = gather(right2_chunk, "x")
    ext, theirs = lax.optimization_barrier((ext, lax.ppermute(right2_chunk, "c", SWAP)))
    ext = lax.all_to_all(ext, ("c", "x", "y", "zh"), 0, 0)
    right2 = mine + [theirs] + [lax.ppermute(m, "c", SWAP) for m in mine[1:]]
    left_out = call(left_result, (*left1, *left2, ml1, ml2, h2), WIDE)
    right_out = call(right_result, (ext, *right2, prior), WIDE, terms=terms)
    return left_out, right_out


def solution(mesh):
    fine = Mesh(np.asarray(mesh.devices).reshape(4, 4, 2, 4, 2), (*DOC, *TERM))
    return jax.shard_map(
        local,
        mesh=fine,
        in_specs=(P(DOC, TERM, None, None), P(DOC, TERM), P(DOC, TERM), P(DOC, TERM), P(None, TERM)),
        out_specs=(P(None, DOC), P(None, TERM)),
        check_vma=False,
    )
```

```python
import functools

import jax
import jax.numpy as jnp
import numpy as np
from jax import lax
from jax.experimental import pallas as pl
from jax.experimental.pallas import tpu as pltpu
from jax.sharding import Mesh
from jax.sharding import PartitionSpec as P

BLK = 128
K = 16
BR = 64
NB = 320
GROUP = 32
SHARERS = 8
DOC = ("zl", "x", "c")
TERM = ("y", "zh")
F32 = jnp.float32
BF = jnp.bfloat16
HI = lax.Precision.HIGHEST
VMEM = pltpu.VMEM
SMEM = pltpu.SMEM
ANY = pl.ANY


def mm(a, b):
    return jnp.dot(a, b, precision=HI, preferred_element_type=F32)


def mmt(a, b):
    return lax.dot_general(a, b, (((1,), (1,)), ((), ())), precision=HI, preferred_element_type=F32)


def inverse_factor(gram):
    lane = lax.broadcasted_iota(jnp.int32, (K, BLK), 1)
    row = lax.broadcasted_iota(jnp.int32, (K, BLK), 0)
    left = columns(gram)
    result = jnp.where(lane == row, 1.0, 0.0)
    scale = jnp.zeros((K, BLK), F32)
    for j in range(K):
        pivot = left[j][j : j + 1, :]
        scale = jnp.where(row == j, lax.rsqrt(pivot), scale)
        if j == K - 1:
            break
        factor = jnp.where(row > j, left[j] * (1.0 / pivot), 0.0)
        result = result - factor * result[j : j + 1, :]
        for k in range(j + 1, K):
            left[k] = left[k] - factor * left[k][j : j + 1, :]
    return (result * scale)[:, 0:K]


def projected(ext, count):
    proj = ext[:, K : 2 * K] / count
    return proj, inverse_factor(ext[:, 0:K] / count - mmt(proj, proj))


def columns(matrix):
    return [jnp.broadcast_to(matrix[:, j : j + 1], (K, BLK)) for j in range(K)]


def combine(cols, piece):
    total = cols[0] * piece[0:1, :]
    for j in range(1, K):
        total = total + cols[j] * piece[j : j + 1, :]
    return total


def parts(value):
    high = value.astype(BF)
    rest = value - high.astype(F32)
    middle = rest.astype(BF)
    low = (rest - middle.astype(F32)).astype(BF)
    return high, middle, low


def stacked(value):
    return jnp.concatenate(parts(value), axis=0)


def split_store(split_ref, index, value):
    high, middle, low = parts(value)
    split_ref[index, 0:16, :] = high
    split_ref[index, 16:32, :] = middle
    split_ref[index, 32:48, :] = low


def each(count, body, unroll=4):
    def step(i, carry):
        body(i)
        return carry

    lax.fori_loop(0, count, step, 0, unroll=unroll)


def split_all(split_ref, base, piece, count):
    each(count, lambda i: split_store(split_ref, base + i, piece[i]), 8)


def cross(left, right):
    return lax.dot_general(left, right, (((1,), (1,)), ((), ())), preferred_element_type=F32)


def fold(wide):
    rows = (wide[32:48, :] + wide[16:32, :]) + wide[0:16, :]
    return (rows[:, 32:48] + rows[:, 16:32]) + rows[:, 0:16]


def pad_lanes(*pieces):
    width = sum(p.shape[1] for p in pieces)
    return jnp.concatenate([*pieces, jnp.zeros((K, BLK - width), F32)], axis=1)


def spin(index, step):
    return jnp.bitwise_and(index - step, 3)


def group_of(base, live, src_ref, tgt_ref, block, split, acc, place, spare):
    spots, values = [], []
    for u in range(GROUP):
        slot = base + u
        wide = jnp.dot(split[src_ref[0, slot]], block(slot), preferred_element_type=F32)
        values.append((wide[32:48, :] + wide[16:32, :]) + wide[0:16, :])
        spots.append(jnp.where(slot < live, place(tgt_ref[0, slot]), spare))
    for spot, value in zip(spots, values):
        acc[spot] += value


def term_place(y):
    def place(target):
        part = jnp.bitwise_and(lax.shift_right_logical(target, 4) - y, 3)
        return part * 17 + jnp.bitwise_and(target, 15)

    return place


def doc_place(x, core):
    def place(target):
        half = jnp.bitwise_xor(lax.shift_right_logical(target, 5), core)
        part = jnp.bitwise_and(lax.shift_right_logical(target, 3) - x, 3)
        return half * 36 + part * 9 + jnp.bitwise_and(target, 7)

    return place


def multiply(live, src_ref, tgt_ref, held, split, acc, place, spare):
    def step(g, carry):
        group_of(g * GROUP, live, src_ref, tgt_ref, lambda s: held[s], split, acc, place, spare)
        return carry

    lax.fori_loop(0, lax.div(live + (GROUP - 1), GROUP), step, 0)


def gram_step(count, value_of, total, unroll=8):
    def step(i, carry):
        value = value_of(i)
        return carry + cross(value, value)

    return lax.fori_loop(0, count, step, total, unroll=unroll)


def first_forward(
    rows_any, cols_any, counts_any, start_any, blocks, o0, o1, o2, o3, held, turned,
    rows, cols, counts, start, split, acc, sems, small_sems,
):
    groups = NB // GROUP
    small = [
        pltpu.make_async_copy(start_any, start, small_sems.at[0]),
        pltpu.make_async_copy(rows_any, rows, small_sems.at[1]),
        pltpu.make_async_copy(cols_any, cols, small_sems.at[2]),
        pltpu.make_async_copy(counts_any, counts, small_sems.at[3]),
    ]
    for copy in small:
        copy.start()
    for i in range(groups):
        part = pl.ds(i * GROUP, GROUP)
        pltpu.make_async_copy(blocks.at[0, part], held.at[part], sems.at[i]).start()
    acc[...] = jnp.zeros_like(acc)
    for copy in small:
        copy.wait()

    def prepare(i):
        value = stacked(start[:, pl.ds(pl.multiple_of(i * BLK, BLK), BLK)])
        split[i] = value
        return value

    ext = pad_lanes(fold(gram_step(BR, prepare, jnp.zeros((48, 48), F32), 16)))
    live = counts[0, 0]
    place = term_place(lax.axis_index("y"))

    def turn(slot):
        value = held[slot].T
        turned[slot] = value
        return value

    def step(i, carry):
        part = pl.ds(i * GROUP, GROUP)
        pltpu.make_async_copy(blocks.at[0, part], held.at[part], sems.at[i]).wait()

        @pl.when(i * GROUP < live)
        def _():
            group_of(i * GROUP, live, cols, rows, turn, split, acc, place, 16)

        return carry

    lax.fori_loop(0, groups, step, 0)
    for k, out in enumerate((o0, o1, o2, o3)):
        out[0:16] = acc[k * 17 : k * 17 + 16]
        out[16] = ext


def forward(rows, cols, counts, r0, r1, r2, r3, w0, w1, w2, w3, turned, o0, o1, o2, o3, split, acc, grams):
    x, core = lax.axis_index("x"), lax.axis_index("c")
    acc[...] = jnp.zeros_like(acc)
    for side, pieces in ((core, (r0, r1, r2, r3)), (1 - core, (w0, w1, w2, w3))):
        for k, piece in enumerate(pieces):
            base = side * 32 + spin(x, k) * 8
            split_all(split, base, piece, 8)
            grams[side * 4 + spin(x, k)] = piece[8]
    multiply(counts[0, 0], cols, rows, turned, split, acc, term_place(lax.axis_index("y")), 16)
    ext = grams[0]
    for i in range(1, 8):
        ext = ext + grams[i]
    for k, out in enumerate((o0, o1, o2, o3)):
        out[0:16] = acc[k * 17 : k * 17 + 16]
        out[16] = ext


def backward(rows, cols, counts, p0, p1, p2, p3, held, own, other, split, acc, grams):
    y = lax.axis_index("y")
    acc[...] = jnp.zeros_like(acc)
    for k, piece in enumerate((p0, p1, p2, p3)):
        base = spin(y, k) * 16
        split_all(split, base, piece, 16)
        grams[spin(y, k)] = piece[16]
    place = doc_place(lax.axis_index("x"), lax.axis_index("c"))
    multiply(counts[0, 0], rows, cols, held, split, acc, place, 8)
    ext = ((grams[0] + grams[1]) + grams[2]) + grams[3]
    for j in range(8):
        acc[j * 9 + 8] = ext
    own[...] = acc[0:36]
    other[...] = acc[36:72]


def left_first(mine, theirs, out, mr0, *, terms):
    inverse = inverse_factor((mine[16] + theirs[16])[:, 0:K] / terms)
    mr0[...] = pad_lanes(inverse)
    cols = columns(inverse)
    gram = jnp.zeros((48, 48), F32)
    for i in range(16):
        value = combine(cols, mine[i] + theirs[i])
        out[i] = value
        wide = stacked(value)
        gram = gram + cross(wide, wide)
    out[16] = pad_lanes(fold(gram))


def zl_total(t0, t1, t2, t3, order):
    zl = lax.axis_index("zl")
    for k, piece in enumerate((t0, t1, t2, t3)):
        order[spin(zl, k)] = piece[...]
    return lambda i: ((order[0, i] + order[1, i]) + order[2, i]) + order[3, i]


def right_first(t0, t1, t2, t3, start, mr0, out, ml1, right0, order, *, docs):
    total = zl_total(t0, t1, t2, t3, order)
    x, core = lax.axis_index("x"), lax.axis_index("c")
    first = (core * 32 + x * 8) * BLK
    inverse = inverse_factor(total(8)[:, 0:K] / docs)
    ml1[...] = pad_lanes(inverse)
    cols_0 = columns(mr0[:, 0:K])
    cols_1 = columns(inverse)
    gram = jnp.zeros((48, 48), F32)
    mixed = jnp.zeros((48, 48), F32)
    for i in range(8):
        source = pl.ds(pl.multiple_of(first + i * BLK, BLK), BLK)
        prior = combine(cols_0, start[:, source])
        right0[i] = prior
        value = combine(cols_1, total(i))
        out[i] = value
        wide = stacked(value)
        gram = gram + cross(wide, wide)
        mixed = mixed + cross(wide, stacked(prior))
    out[8] = pad_lanes(fold(gram), fold(mixed))


def left_second(mine, theirs, left_raw, ml1, out, mr1, h1, *, terms):
    proj, inverse = projected(mine[16] + theirs[16], terms)
    mr1[...] = pad_lanes(inverse)
    h1[...] = pad_lanes(proj)
    cols_l = columns(ml1[:, 0:K])
    cols_h = columns(proj)
    for i in range(16):
        out[i] = (mine[i] + theirs[i]) - combine(cols_h, left_raw[i])
    cols_m = columns(inverse)
    gram = jnp.zeros((48, 48), F32)
    mixed = jnp.zeros((48, 48), F32)
    for i in range(16):
        prior = stacked(combine(cols_l, left_raw[i]))
        value = combine(cols_m, out[i])
        out[i] = value
        wide = stacked(value)
        gram = gram + cross(wide, wide)
        mixed = mixed + cross(wide, prior)
    out[16] = pad_lanes(fold(gram), fold(mixed))


def right_second(t0, t1, t2, t3, right_raw, prior, out, ml2, h2, order, *, docs):
    total = zl_total(t0, t1, t2, t3, order)
    first = lax.axis_index("c") * 32 + lax.axis_index("x") * 8
    proj, inverse = projected(total(8), docs)
    ml2[...] = pad_lanes(inverse)
    h2[...] = pad_lanes(proj)
    cols_h = columns(proj)
    for i in range(8):
        out[i] = total(i) - combine(cols_h, right_raw[i])
    cols_m = columns(inverse)
    gram = jnp.zeros((48, 48), F32)
    mixed = jnp.zeros((48, 48), F32)
    for i in range(8):
        value = combine(cols_m, out[i])
        out[i] = value
        wide = stacked(value)
        gram = gram + cross(wide, wide)
        mixed = mixed + cross(wide, prior[first + i])
    out[8] = pad_lanes(fold(gram), fold(mixed))


def gram_copies(r0, r1, r2, r3, w0, w1, w2, w3, ext_out, grams):
    for base, piece in by_side((r0, r1, r2, r3, w0, w1, w2, w3)):
        grams[lax.shift_right_logical(base, 3)] = piece[8]
    total = grams[0]
    for i in range(1, 8):
        total = total + grams[i]
    packed = jnp.concatenate([total[0:8, 0 : 2 * K], total[8:16, 0 : 2 * K], jnp.zeros((8, BLK - 4 * K), F32)], axis=1)
    for i in range(SHARERS):
        ext_out[i] = packed


def lanes(index):
    return pl.ds(pl.multiple_of(index * BLK, BLK), BLK)


def factor_parts(*matrices):
    tall = [jnp.concatenate([p.astype(F32) for p in parts(m)], axis=0) for m in matrices]
    return jnp.concatenate([t for t in tall for _ in range(3)], axis=1).astype(BF)


def mix(factors, first, second):
    wide = jnp.dot(factors, jnp.concatenate([first, second], axis=0), preferred_element_type=F32)
    return (wide[32:48, :] + wide[16:32, :]) + wide[0:16, :]


def left_result(a0, a1, a2, a3, b0, b1, b2, b3, ml1, ml2, h2, out):
    y = lax.axis_index("y")
    inverse = ml2[:, 0:K]
    factors = factor_parts(inverse, -mm(mm(inverse, h2[:, 0:K]), ml1[:, 0:K]))
    for k, (first, second) in enumerate(zip((a0, a1, a2, a3), (b0, b1, b2, b3))):
        base = spin(y, k) * 16

        def result(i, base=base, first=first, second=second):
            out[:, lanes(base + i)] = mix(factors, stacked(second[i]), stacked(first[i]))

        each(16, result, 8)


def by_side(pieces):
    x, core = lax.axis_index("x"), lax.axis_index("c")
    for n, piece in enumerate(pieces):
        side = core if n < 4 else 1 - core
        yield side * 32 + spin(x, n % 4) * 8, piece


def right_prior(r0, r1, r2, r3, w0, w1, w2, w3, start, mr0, mr1, h1, out, work):
    cols_0 = columns(mr0[:, 0:K])

    def from_start(i):
        work[i] = combine(cols_0, start[:, lanes(i)])

    each(BR, from_start)
    cols_h = columns(h1[:, 0:K])
    for base, piece in by_side((r0, r1, r2, r3, w0, w1, w2, w3)):

        def rest(i, base=base, piece=piece):
            work[base + i] = piece[i] - combine(cols_h, work[base + i])

        each(8, rest)
    cols_1 = columns(mr1[:, 0:K])

    def final(i):
        split_store(out, i, combine(cols_1, work[i]))

    each(BR, final)


def right_result(ext, r0, r1, r2, r3, w0, w1, w2, w3, right1, out, *, terms):
    total = ext[0]
    for i in range(1, SHARERS):
        total = total + ext[i]
    both = jnp.concatenate([total[:, 0 : 2 * K], total[:, 2 * K : 4 * K]], axis=0)
    proj, inverse = projected(both, terms)
    factors = factor_parts(inverse, -mm(inverse, proj))
    for base, piece in by_side((r0, r1, r2, r3, w0, w1, w2, w3)):

        def result(i, base=base, piece=piece):
            out[:, lanes(base + i)] = mix(factors, stacked(piece[i]), right1[base + i])

        each(8, result, 8)


def panel(n):
    return jax.ShapeDtypeStruct((n, K, BLK), F32)


SMALL = jax.ShapeDtypeStruct((K, BLK), F32)
WIDE = jax.ShapeDtypeStruct((K, BR * BLK), F32)
TILE = jax.ShapeDtypeStruct((NB, BLK, BLK), BF)
SPLIT = VMEM((BR, 48, BLK), BF)


def held_panel(n):
    return VMEM((n, K, BLK), F32)


def call(body, args, outs, scratch=(), spaces=None, limit=8, micros=2, **constants):
    def space(a):
        return SMEM if a.dtype == jnp.int32 else VMEM

    spaces = spaces or [space(a) for a in args]
    return pl.pallas_call(
        functools.partial(body, **constants) if constants else body,
        name=body.__name__,
        out_shape=outs,
        in_specs=[pl.BlockSpec(memory_space=s) for s in spaces],
        out_specs=jax.tree.map(lambda _: pl.BlockSpec(memory_space=VMEM), outs),
        scratch_shapes=list(scratch),
        cost_estimate=pl.CostEstimate(
            flops=micros * 1000000000, bytes_accessed=micros * 1000000, transcendentals=0
        ),
        compiler_params=pltpu.CompilerParams(vmem_limit_bytes=limit * 1024 * 1024),
    )(*args)


SWAP = [(0, 1), (1, 0)]


def shift(value, axis, k):
    return lax.ppermute(value, axis, [(i, (i + k) % 4) for i in range(4)])


def gather(value, axis):
    return [value] + [shift(value, axis, k) for k in (1, 2, 3)]


def total_of(got):
    return ((got[0] + got[1]) + got[2]) + got[3]


def scatter_term(pieces):
    got = [pieces[0]] + [shift(pieces[k], "y", k) for k in (1, 2, 3)]
    mine = total_of(got)
    return mine, lax.ppermute(mine, "zh", SWAP)


def scatter_doc(own, other):
    got = lax.ppermute(other, "c", SWAP)
    pieces = [own[9 * k : 9 * k + 9] + got[9 * k : 9 * k + 9] for k in range(4)]
    got = [pieces[0]] + [shift(pieces[k], "x", k) for k in (1, 2, 3)]
    return gather(total_of(got), "zl")


def gather_doc(value):
    mine = gather(value, "x")
    return mine + [lax.ppermute(m, "c", SWAP) for m in mine]


def local(blocks, block_rows, block_cols, counts, start):
    docs = float(BR * BLK * 32)
    terms = float(BR * BLK * 8)
    index = (block_rows, block_cols, counts)

    *pieces, held, turned = call(
        first_forward,
        (*index, start, blocks),
        (panel(17),) * 4 + (TILE, TILE),
        [
            SMEM((1, NB), jnp.int32), SMEM((1, NB), jnp.int32), SMEM((1, 1), jnp.int32),
            VMEM((K, BR * BLK), F32), SPLIT, held_panel(68),
            pltpu.SemaphoreType.DMA((NB // GROUP,)), pltpu.SemaphoreType.DMA((4,)),
        ],
        spaces=[pltpu.HBM] * 5,
        limit=30,
    )
    left_chunk, mr0 = call(left_first, scatter_term(pieces), (panel(17), SMALL), terms=terms)
    left1 = gather(left_chunk, "y")
    back_scratch = [SPLIT, held_panel(72), held_panel(4)]
    own, other = call(backward, (*index, *left1, held), (panel(36), panel(36)), back_scratch, limit=20)
    right_chunk, ml1, right0 = call(
        right_first, (*scatter_doc(own, other), start, mr0), (panel(9), SMALL, panel(8)),
        [VMEM((4, 9, K, BLK), F32)], docs=docs,
    )
    right1 = gather_doc(right_chunk)
    pieces = call(
        forward, (*index, *right1, turned), (panel(17),) * 4, [SPLIT, held_panel(68), held_panel(8)], limit=20
    )
    left2_chunk, mr1, h1 = call(
        left_second, (*scatter_term(pieces), left_chunk, ml1), (panel(17), SMALL, SMALL), terms=terms
    )
    left2 = gather(left2_chunk, "y")
    own, other = call(backward, (*index, *left2, held), (panel(36), panel(36)), back_scratch, limit=20)
    prior = call(
        right_prior, (*right1, start, mr0, mr1, h1), jax.ShapeDtypeStruct((BR, 48, BLK), BF), [held_panel(BR)]
    )
    right2_chunk, ml2, h2 = call(
        right_second, (*scatter_doc(own, other), right_chunk, prior), (panel(9), SMALL, SMALL),
        [VMEM((4, 9, K, BLK), F32)], docs=docs,
    )
    left_out = call(left_result, (*left1, *left2, ml1, ml2, h2), WIDE)
    mine = gather(right2_chunk, "x")
    mine[3], left_out = lax.optimization_barrier((mine[3], left_out))
    right2 = mine + [lax.ppermute(m, "c", SWAP) for m in mine]
    ext = call(gram_copies, right2, jax.ShapeDtypeStruct((SHARERS, 8, BLK), F32), [held_panel(8)])
    ext = lax.all_to_all(ext, TERM, 0, 0)
    right_out = call(right_result, (ext, *right2, prior), WIDE, terms=terms)
    return left_out, right_out


def solution(mesh):
    fine = Mesh(np.asarray(mesh.devices).reshape(4, 4, 2, 4, 2), (*DOC, *TERM))
    return jax.shard_map(
        local,
        mesh=fine,
        in_specs=(P(DOC, TERM, None, None), P(DOC, TERM), P(DOC, TERM), P(DOC, TERM), P(None, TERM)),
        out_specs=(P(None, DOC), P(None, TERM)),
        check_vma=False,
    )
```

```python
import functools

import jax
import jax.numpy as jnp
import numpy as np
from jax import lax
from jax.experimental import pallas as pl
from jax.experimental.pallas import tpu as pltpu
from jax.sharding import Mesh
from jax.sharding import PartitionSpec as P

BLK = 128
K = 16
BR = 64
NB = 320
GROUP = 32
SHARERS = 64
DOC = ("zl", "x", "c")
TERM = ("y", "zh")
F32 = jnp.float32
BF = jnp.bfloat16
HI = lax.Precision.HIGHEST
VMEM = pltpu.VMEM
SMEM = pltpu.SMEM
ANY = pl.ANY


def mm(a, b):
    return jnp.dot(a, b, precision=HI, preferred_element_type=F32)


def mmt(a, b):
    return lax.dot_general(a, b, (((1,), (1,)), ((), ())), precision=HI, preferred_element_type=F32)


def inverse_factor(gram):
    lane = lax.broadcasted_iota(jnp.int32, (K, BLK), 1)
    row = lax.broadcasted_iota(jnp.int32, (K, BLK), 0)
    left = columns(gram)
    result = jnp.where(lane == row, 1.0, 0.0)
    scale = jnp.zeros((K, BLK), F32)
    for j in range(K):
        pivot = left[j][j : j + 1, :]
        scale = jnp.where(row == j, lax.rsqrt(pivot), scale)
        if j == K - 1:
            break
        factor = jnp.where(row > j, left[j] * (1.0 / pivot), 0.0)
        result = result - factor * result[j : j + 1, :]
        for k in range(j + 1, K):
            left[k] = left[k] - factor * left[k][j : j + 1, :]
    return (result * scale)[:, 0:K]


def projected(ext, count):
    proj = ext[:, K : 2 * K] / count
    return proj, inverse_factor(ext[:, 0:K] / count - mmt(proj, proj))


def columns(matrix):
    return [jnp.broadcast_to(matrix[:, j : j + 1], (K, BLK)) for j in range(K)]


def combine(cols, piece):
    total = cols[0] * piece[0:1, :]
    for j in range(1, K):
        total = total + cols[j] * piece[j : j + 1, :]
    return total


def parts(value):
    high = value.astype(BF)
    rest = value - high.astype(F32)
    middle = rest.astype(BF)
    low = (rest - middle.astype(F32)).astype(BF)
    return high, middle, low


def stacked(value):
    return jnp.concatenate(parts(value), axis=0)


def split_store(split_ref, index, value):
    high, middle, low = parts(value)
    split_ref[index, 0:16, :] = high
    split_ref[index, 16:32, :] = middle
    split_ref[index, 32:48, :] = low


def each(count, body, unroll=4):
    def step(i, carry):
        body(i)
        return carry

    lax.fori_loop(0, count, step, 0, unroll=unroll)


def split_all(split_ref, base, piece, count):
    each(count, lambda i: split_store(split_ref, base + i, piece[i]), 8)


def cross(left, right):
    return lax.dot_general(left, right, (((1,), (1,)), ((), ())), preferred_element_type=F32)


def fold(wide):
    rows = (wide[32:48, :] + wide[16:32, :]) + wide[0:16, :]
    return (rows[:, 32:48] + rows[:, 16:32]) + rows[:, 0:16]


def pad_lanes(*pieces):
    width = sum(p.shape[1] for p in pieces)
    return jnp.concatenate([*pieces, jnp.zeros((K, BLK - width), F32)], axis=1)


def spin(index, step):
    return jnp.bitwise_and(index - step, 3)


def group_of(base, live, src_ref, tgt_ref, block, split, acc, place, spare):
    spots, values = [], []
    for u in range(GROUP):
        slot = base + u
        wide = jnp.dot(split[src_ref[0, slot]], block(slot), preferred_element_type=F32)
        values.append((wide[32:48, :] + wide[16:32, :]) + wide[0:16, :])
        spots.append(jnp.where(slot < live, place(tgt_ref[0, slot]), spare))
    for spot, value in zip(spots, values):
        acc[spot] += value


def term_place(y):
    def place(target):
        part = jnp.bitwise_and(lax.shift_right_logical(target, 4) - y, 3)
        return part * 17 + jnp.bitwise_and(target, 15)

    return place


def doc_place(x, core):
    def place(target):
        half = jnp.bitwise_xor(lax.shift_right_logical(target, 5), core)
        part = jnp.bitwise_and(lax.shift_right_logical(target, 3) - x, 3)
        return half * 36 + part * 9 + jnp.bitwise_and(target, 7)

    return place


def multiply(live, src_ref, tgt_ref, held, split, acc, place, spare):
    def step(g, carry):
        group_of(g * GROUP, live, src_ref, tgt_ref, lambda s: held[s], split, acc, place, spare)
        return carry

    lax.fori_loop(0, lax.div(live + (GROUP - 1), GROUP), step, 0)


def gram_step(count, value_of, total, unroll=8):
    def step(i, carry):
        value = value_of(i)
        return carry + cross(value, value)

    return lax.fori_loop(0, count, step, total, unroll=unroll)


def first_forward(
    rows_any, cols_any, counts_any, start_any, blocks, o0, o1, o2, o3, held, turned,
    rows, cols, counts, start, split, acc, sems, small_sems,
):
    groups = NB // GROUP
    small = [
        pltpu.make_async_copy(start_any, start, small_sems.at[0]),
        pltpu.make_async_copy(rows_any, rows, small_sems.at[1]),
        pltpu.make_async_copy(cols_any, cols, small_sems.at[2]),
        pltpu.make_async_copy(counts_any, counts, small_sems.at[3]),
    ]
    for copy in small:
        copy.start()
    for i in range(groups):
        part = pl.ds(i * GROUP, GROUP)
        pltpu.make_async_copy(blocks.at[0, part], held.at[part], sems.at[i]).start()
    acc[...] = jnp.zeros_like(acc)
    for copy in small:
        copy.wait()

    def prepare(i):
        value = stacked(start[:, pl.ds(pl.multiple_of(i * BLK, BLK), BLK)])
        split[i] = value
        return value

    ext = pad_lanes(fold(gram_step(BR, prepare, jnp.zeros((48, 48), F32), 16)))
    live = counts[0, 0]
    place = term_place(lax.axis_index("y"))

    def turn(slot):
        value = held[slot].T
        turned[slot] = value
        return value

    def step(i, carry):
        part = pl.ds(i * GROUP, GROUP)
        pltpu.make_async_copy(blocks.at[0, part], held.at[part], sems.at[i]).wait()

        @pl.when(i * GROUP < live)
        def _():
            group_of(i * GROUP, live, cols, rows, turn, split, acc, place, 16)

        return carry

    lax.fori_loop(0, groups, step, 0)
    for k, out in enumerate((o0, o1, o2, o3)):
        out[0:16] = acc[k * 17 : k * 17 + 16]
        out[16] = ext


def forward(rows, cols, counts, r0, r1, r2, r3, w0, w1, w2, w3, turned, o0, o1, o2, o3, split, acc, grams):
    x, core = lax.axis_index("x"), lax.axis_index("c")
    acc[...] = jnp.zeros_like(acc)
    for side, pieces in ((core, (r0, r1, r2, r3)), (1 - core, (w0, w1, w2, w3))):
        for k, piece in enumerate(pieces):
            base = side * 32 + spin(x, k) * 8
            split_all(split, base, piece, 8)
            grams[side * 4 + spin(x, k)] = piece[8]
    multiply(counts[0, 0], cols, rows, turned, split, acc, term_place(lax.axis_index("y")), 16)
    ext = grams[0]
    for i in range(1, 8):
        ext = ext + grams[i]
    for k, out in enumerate((o0, o1, o2, o3)):
        out[0:16] = acc[k * 17 : k * 17 + 16]
        out[16] = ext


def backward(rows, cols, counts, p0, p1, p2, p3, held, own, other, split, acc, grams):
    y = lax.axis_index("y")
    acc[...] = jnp.zeros_like(acc)
    for k, piece in enumerate((p0, p1, p2, p3)):
        base = spin(y, k) * 16
        split_all(split, base, piece, 16)
        grams[spin(y, k)] = piece[16]
    place = doc_place(lax.axis_index("x"), lax.axis_index("c"))
    multiply(counts[0, 0], rows, cols, held, split, acc, place, 8)
    ext = ((grams[0] + grams[1]) + grams[2]) + grams[3]
    for j in range(8):
        acc[j * 9 + 8] = ext
    own[...] = acc[0:36]
    other[...] = acc[36:72]


def left_first(mine, theirs, out, mr0, *, terms):
    inverse = inverse_factor((mine[16] + theirs[16])[:, 0:K] / terms)
    mr0[...] = pad_lanes(inverse)
    cols = columns(inverse)
    gram = jnp.zeros((48, 48), F32)
    for i in range(16):
        value = combine(cols, mine[i] + theirs[i])
        out[i] = value
        wide = stacked(value)
        gram = gram + cross(wide, wide)
    out[16] = pad_lanes(fold(gram))


def zl_total(t0, t1, t2, t3, order):
    zl = lax.axis_index("zl")
    for k, piece in enumerate((t0, t1, t2, t3)):
        order[spin(zl, k)] = piece[...]
    return lambda i: ((order[0, i] + order[1, i]) + order[2, i]) + order[3, i]


def right_first(t0, t1, t2, t3, start, mr0, out, ml1, right0, order, *, docs):
    total = zl_total(t0, t1, t2, t3, order)
    x, core = lax.axis_index("x"), lax.axis_index("c")
    first = (core * 32 + x * 8) * BLK
    inverse = inverse_factor(total(8)[:, 0:K] / docs)
    ml1[...] = pad_lanes(inverse)
    cols_0 = columns(mr0[:, 0:K])
    cols_1 = columns(inverse)
    gram = jnp.zeros((48, 48), F32)
    mixed = jnp.zeros((48, 48), F32)
    for i in range(8):
        source = pl.ds(pl.multiple_of(first + i * BLK, BLK), BLK)
        prior = combine(cols_0, start[:, source])
        right0[i] = prior
        value = combine(cols_1, total(i))
        out[i] = value
        wide = stacked(value)
        gram = gram + cross(wide, wide)
        mixed = mixed + cross(wide, stacked(prior))
    out[8] = pad_lanes(fold(gram), fold(mixed))


def left_second(mine, theirs, left_raw, ml1, out, mr1, h1, *, terms):
    proj, inverse = projected(mine[16] + theirs[16], terms)
    mr1[...] = pad_lanes(inverse)
    h1[...] = pad_lanes(proj)
    cols_l = columns(ml1[:, 0:K])
    cols_h = columns(proj)
    for i in range(16):
        out[i] = (mine[i] + theirs[i]) - combine(cols_h, left_raw[i])
    cols_m = columns(inverse)
    gram = jnp.zeros((48, 48), F32)
    mixed = jnp.zeros((48, 48), F32)
    for i in range(16):
        prior = stacked(combine(cols_l, left_raw[i]))
        value = combine(cols_m, out[i])
        out[i] = value
        wide = stacked(value)
        gram = gram + cross(wide, wide)
        mixed = mixed + cross(wide, prior)
    out[16] = pad_lanes(fold(gram), fold(mixed))


def right_second(t0, t1, t2, t3, right_raw, prior, out, ext_out, ml2, h2, order, *, docs):
    total = zl_total(t0, t1, t2, t3, order)
    first = lax.axis_index("c") * 32 + lax.axis_index("x") * 8
    proj, inverse = projected(total(8), docs)
    ml2[...] = pad_lanes(inverse)
    h2[...] = pad_lanes(proj)
    cols_h = columns(proj)
    for i in range(8):
        out[i] = total(i) - combine(cols_h, right_raw[i])
    cols_m = columns(inverse)
    gram = jnp.zeros((48, 48), F32)
    mixed = jnp.zeros((48, 48), F32)
    for i in range(8):
        value = combine(cols_m, out[i])
        out[i] = value
        wide = stacked(value)
        gram = gram + cross(wide, wide)
        mixed = mixed + cross(wide, prior[first + i])
    both = jnp.concatenate([fold(gram), fold(mixed)], axis=1)
    ext_out[...] = jnp.broadcast_to(
        jnp.concatenate([both[0:8], both[8:16], jnp.zeros((8, 64), F32)], axis=1)[None], (SHARERS, 8, BLK)
    )


def lanes(index):
    return pl.ds(pl.multiple_of(index * BLK, BLK), BLK)


def factor_parts(*matrices):
    tall = [jnp.concatenate([p.astype(F32) for p in parts(m)], axis=0) for m in matrices]
    return jnp.concatenate([t for t in tall for _ in range(3)], axis=1).astype(BF)


def mix(factors, first, second):
    wide = jnp.dot(factors, jnp.concatenate([first, second], axis=0), preferred_element_type=F32)
    return (wide[32:48, :] + wide[16:32, :]) + wide[0:16, :]


def left_result(first, second, ml1, ml2, h2, out):
    inverse = ml2[:, 0:K]
    factors = factor_parts(inverse, -mm(mm(inverse, h2[:, 0:K]), ml1[:, 0:K]))

    def result(i):
        out[:, lanes(i)] = mix(factors, second[i], first[i])

    each(BR, result, 8)


def by_side(pieces):
    x, core = lax.axis_index("x"), lax.axis_index("c")
    for n, piece in enumerate(pieces):
        side = core if n < 4 else 1 - core
        yield side * 32 + spin(x, n % 4) * 8, piece


def right_prior(r0, r1, r2, r3, w0, w1, w2, w3, start, mr0, mr1, h1, out, work):
    cols_0 = columns(mr0[:, 0:K])

    def from_start(i):
        work[i] = combine(cols_0, start[:, lanes(i)])

    each(BR, from_start)
    cols_h = columns(h1[:, 0:K])
    for base, piece in by_side((r0, r1, r2, r3, w0, w1, w2, w3)):

        def rest(i, base=base, piece=piece):
            work[base + i] = piece[i] - combine(cols_h, work[base + i])

        each(8, rest)
    cols_1 = columns(mr1[:, 0:K])

    def final(i):
        split_store(out, i, combine(cols_1, work[i]))

    each(BR, final)


def right_result(ext, r0, r1, r2, r3, w0, w1, w2, w3, right1, out, *, terms):
    total = ext[0]
    for i in range(1, SHARERS):
        total = total + ext[i]
    both = jnp.concatenate([total[:, 0 : 2 * K], total[:, 2 * K : 4 * K]], axis=0)
    proj, inverse = projected(both, terms)
    factors = factor_parts(inverse, -mm(inverse, proj))
    for base, piece in by_side((r0, r1, r2, r3, w0, w1, w2, w3)):

        def result(i, base=base, piece=piece):
            out[:, lanes(base + i)] = mix(factors, stacked(piece[i]), right1[base + i])

        each(8, result, 8)


def panel(n):
    return jax.ShapeDtypeStruct((n, K, BLK), F32)


SMALL = jax.ShapeDtypeStruct((K, BLK), F32)
WIDE = jax.ShapeDtypeStruct((K, BR * BLK), F32)
TILE = jax.ShapeDtypeStruct((NB, BLK, BLK), BF)
PARTS = jax.ShapeDtypeStruct((BR, 48, BLK), BF)
SPLIT = VMEM((BR, 48, BLK), BF)


def held_panel(n):
    return VMEM((n, K, BLK), F32)


def call(body, args, outs, scratch=(), spaces=None, limit=8, micros=2, **constants):
    def space(a):
        return SMEM if a.dtype == jnp.int32 else VMEM

    spaces = spaces or [space(a) for a in args]
    return pl.pallas_call(
        functools.partial(body, **constants) if constants else body,
        name=body.__name__,
        out_shape=outs,
        in_specs=[pl.BlockSpec(memory_space=s) for s in spaces],
        out_specs=jax.tree.map(lambda _: pl.BlockSpec(memory_space=VMEM), outs),
        scratch_shapes=list(scratch),
        cost_estimate=pl.CostEstimate(
            flops=micros * 1000000000, bytes_accessed=micros * 1000000, transcendentals=0
        ),
        compiler_params=pltpu.CompilerParams(vmem_limit_bytes=limit * 1024 * 1024),
    )(*args)


SWAP = [(0, 1), (1, 0)]


def shift(value, axis, k):
    return lax.ppermute(value, axis, [(i, (i + k) % 4) for i in range(4)])


def gather(value, axis):
    return [value] + [shift(value, axis, k) for k in (1, 2, 3)]


def total_of(got):
    return ((got[0] + got[1]) + got[2]) + got[3]


def scatter_term(pieces):
    got = [pieces[0]] + [shift(pieces[k], "y", k) for k in (1, 2, 3)]
    mine = total_of(got)
    return mine, lax.ppermute(mine, "zh", SWAP)


def scatter_doc(own, other):
    got = lax.ppermute(other, "c", SWAP)
    pieces = [own[9 * k : 9 * k + 9] + got[9 * k : 9 * k + 9] for k in range(4)]
    got = [pieces[0]] + [shift(pieces[k], "x", k) for k in (1, 2, 3)]
    return gather(total_of(got), "zl")


def gather_doc(value):
    mine = gather(value, "x")
    return mine + [lax.ppermute(m, "c", SWAP) for m in mine]


def local(blocks, block_rows, block_cols, counts, start):
    docs = float(BR * BLK * 32)
    terms = float(BR * BLK * 8)
    index = (block_rows, block_cols, counts)

    *pieces, held, turned = call(
        first_forward,
        (*index, start, blocks),
        (panel(17),) * 4 + (TILE, TILE),
        [
            SMEM((1, NB), jnp.int32), SMEM((1, NB), jnp.int32), SMEM((1, 1), jnp.int32),
            VMEM((K, BR * BLK), F32), SPLIT, held_panel(68),
            pltpu.SemaphoreType.DMA((NB // GROUP,)), pltpu.SemaphoreType.DMA((4,)),
        ],
        spaces=[pltpu.HBM] * 5,
        limit=30,
    )
    left_chunk, mr0 = call(left_first, scatter_term(pieces), (panel(17), SMALL), terms=terms)
    left1 = gather(left_chunk, "y")
    back_scratch = [held_panel(72), held_panel(4)]
    back_outs = (panel(36), panel(36), PARTS)
    own, other, left1_parts = call(backward, (*index, *left1, held), back_outs, back_scratch, limit=20)
    right_chunk, ml1, right0 = call(
        right_first, (*scatter_doc(own, other), start, mr0), (panel(9), SMALL, panel(8)),
        [VMEM((4, 9, K, BLK), F32)], docs=docs,
    )
    right1 = gather_doc(right_chunk)
    pieces = call(
        forward, (*index, *right1, turned), (panel(17),) * 4, [SPLIT, held_panel(68), held_panel(8)], limit=20
    )
    left2_chunk, mr1, h1 = call(
        left_second, (*scatter_term(pieces), left_chunk, ml1), (panel(17), SMALL, SMALL), terms=terms
    )
    left2 = gather(left2_chunk, "y")
    own, other, left2_parts = call(backward, (*index, *left2, held), back_outs, back_scratch, limit=20)
    prior = call(
        right_prior, (*right1, start, mr0, mr1, h1), PARTS, [held_panel(BR)]
    )
    right2_chunk, ext, ml2, h2 = call(
        right_second, (*scatter_doc(own, other), right_chunk, prior),
        (panel(8), jax.ShapeDtypeStruct((SHARERS, 8, BLK), F32), SMALL, SMALL),
        [VMEM((4, 9, K, BLK), F32)], docs=docs,
    )
    mine = gather(right2_chunk, "x")
    left_out = call(left_result, (left1_parts, left2_parts, ml1, ml2, h2), WIDE)
    ext, left_out, *mine = lax.optimization_barrier((ext, left_out, *mine))
    ext = lax.all_to_all(ext, ("c", "x", "y", "zh"), 0, 0)
    right2 = mine + [lax.ppermute(m, "c", SWAP) for m in mine]
    right_out = call(right_result, (ext, *right2, prior), WIDE, terms=terms)
    return left_out, right_out


def solution(mesh):
    fine = Mesh(np.asarray(mesh.devices).reshape(4, 4, 2, 4, 2), (*DOC, *TERM))
    return jax.shard_map(
        local,
        mesh=fine,
        in_specs=(P(DOC, TERM, None, None), P(DOC, TERM), P(DOC, TERM), P(DOC, TERM), P(None, TERM)),
        out_specs=(P(None, DOC), P(None, TERM)),
        check_vma=False,
    )
```

```python
import functools

import jax
import jax.numpy as jnp
import numpy as np
from jax import lax
from jax.experimental import pallas as pl
from jax.experimental.pallas import tpu as pltpu
from jax.sharding import Mesh
from jax.sharding import PartitionSpec as P

BLK = 128
K = 16
BR = 64
NB = 320
GROUP = 32
SHARERS = 64
DOC = ("zl", "x", "c")
TERM = ("y", "zh")
F32 = jnp.float32
BF = jnp.bfloat16
HI = lax.Precision.HIGHEST
VMEM = pltpu.VMEM
SMEM = pltpu.SMEM
ANY = pl.ANY


def mm(a, b):
    return jnp.dot(a, b, precision=HI, preferred_element_type=F32)


def mmt(a, b):
    return lax.dot_general(a, b, (((1,), (1,)), ((), ())), precision=HI, preferred_element_type=F32)


def inverse_factor(gram):
    lane = lax.broadcasted_iota(jnp.int32, (K, BLK), 1)
    row = lax.broadcasted_iota(jnp.int32, (K, BLK), 0)
    left = columns(gram)
    result = jnp.where(lane == row, 1.0, 0.0)
    scale = jnp.zeros((K, BLK), F32)
    for j in range(K):
        pivot = left[j][j : j + 1, :]
        scale = jnp.where(row == j, lax.rsqrt(pivot), scale)
        if j == K - 1:
            break
        factor = jnp.where(row > j, left[j] * (1.0 / pivot), 0.0)
        result = result - factor * result[j : j + 1, :]
        for k in range(j + 1, K):
            left[k] = left[k] - factor * left[k][j : j + 1, :]
    return (result * scale)[:, 0:K]


def projected(ext, count):
    proj = ext[:, K : 2 * K] / count
    return proj, inverse_factor(ext[:, 0:K] / count - mmt(proj, proj))


def columns(matrix):
    return [jnp.broadcast_to(matrix[:, j : j + 1], (K, BLK)) for j in range(K)]


def combine(cols, piece):
    total = cols[0] * piece[0:1, :]
    for j in range(1, K):
        total = total + cols[j] * piece[j : j + 1, :]
    return total


def parts(value):
    high = value.astype(BF)
    rest = value - high.astype(F32)
    middle = rest.astype(BF)
    low = (rest - middle.astype(F32)).astype(BF)
    return high, middle, low


def stacked(value):
    return jnp.concatenate(parts(value), axis=0)


def split_store(split_ref, index, value):
    high, middle, low = parts(value)
    split_ref[index, 0:16, :] = high
    split_ref[index, 16:32, :] = middle
    split_ref[index, 32:48, :] = low


def each(count, body, unroll=4):
    def step(i, carry):
        body(i)
        return carry

    lax.fori_loop(0, count, step, 0, unroll=unroll)


def split_all(split_ref, base, piece, count):
    each(count, lambda i: split_store(split_ref, base + i, piece[i]), 8)


def cross(left, right):
    return lax.dot_general(left, right, (((1,), (1,)), ((), ())), preferred_element_type=F32)


def fold(wide):
    rows = (wide[32:48, :] + wide[16:32, :]) + wide[0:16, :]
    return (rows[:, 32:48] + rows[:, 16:32]) + rows[:, 0:16]


def pad_lanes(*pieces):
    width = sum(p.shape[1] for p in pieces)
    return jnp.concatenate([*pieces, jnp.zeros((K, BLK - width), F32)], axis=1)


def spin(index, step):
    return jnp.bitwise_and(index - step, 3)


def group_of(base, live, src_ref, tgt_ref, block, split, acc, place, spare):
    spots, values = [], []
    for u in range(GROUP):
        slot = base + u
        wide = jnp.dot(split[src_ref[0, slot]], block(slot), preferred_element_type=F32)
        values.append((wide[32:48, :] + wide[16:32, :]) + wide[0:16, :])
        spots.append(jnp.where(slot < live, place(tgt_ref[0, slot]), spare))
    for spot, value in zip(spots, values):
        acc[spot] += value


def term_place(y):
    def place(target):
        part = jnp.bitwise_and(lax.shift_right_logical(target, 4) - y, 3)
        return part * 17 + jnp.bitwise_and(target, 15)

    return place


def doc_place(x, core):
    def place(target):
        half = jnp.bitwise_xor(lax.shift_right_logical(target, 5), core)
        part = jnp.bitwise_and(lax.shift_right_logical(target, 3) - x, 3)
        return half * 36 + part * 9 + jnp.bitwise_and(target, 7)

    return place


def multiply(live, src_ref, tgt_ref, held, split, acc, place, spare):
    def step(g, carry):
        group_of(g * GROUP, live, src_ref, tgt_ref, lambda s: held[s], split, acc, place, spare)
        return carry

    lax.fori_loop(0, lax.div(live + (GROUP - 1), GROUP), step, 0)


def gram_step(count, value_of, total, unroll=8):
    def step(i, carry):
        value = value_of(i)
        return carry + cross(value, value)

    return lax.fori_loop(0, count, step, total, unroll=unroll)


def first_forward(
    rows_any, cols_any, counts_any, start_any, blocks, o0, o1, o2, o3, held, turned,
    rows, cols, counts, start, split, acc, sems, small_sems,
):
    groups = NB // GROUP
    small = [
        pltpu.make_async_copy(start_any, start, small_sems.at[0]),
        pltpu.make_async_copy(rows_any, rows, small_sems.at[1]),
        pltpu.make_async_copy(cols_any, cols, small_sems.at[2]),
        pltpu.make_async_copy(counts_any, counts, small_sems.at[3]),
    ]
    for copy in small:
        copy.start()
    for i in range(groups):
        part = pl.ds(i * GROUP, GROUP)
        pltpu.make_async_copy(blocks.at[0, part], held.at[part], sems.at[i]).start()
    acc[...] = jnp.zeros_like(acc)
    for copy in small:
        copy.wait()

    def prepare(i):
        value = stacked(start[:, pl.ds(pl.multiple_of(i * BLK, BLK), BLK)])
        split[i] = value
        return value

    ext = pad_lanes(fold(gram_step(BR, prepare, jnp.zeros((48, 48), F32), 16)))
    live = counts[0, 0]
    place = term_place(lax.axis_index("y"))

    def turn(slot):
        value = held[slot].T
        turned[slot] = value
        return value

    def step(i, carry):
        part = pl.ds(i * GROUP, GROUP)
        pltpu.make_async_copy(blocks.at[0, part], held.at[part], sems.at[i]).wait()

        @pl.when(i * GROUP < live)
        def _():
            group_of(i * GROUP, live, cols, rows, turn, split, acc, place, 16)

        return carry

    lax.fori_loop(0, groups, step, 0)
    for k, out in enumerate((o0, o1, o2, o3)):
        out[0:16] = acc[k * 17 : k * 17 + 16]
        out[16] = ext


def forward(rows, cols, counts, r0, r1, r2, r3, w0, w1, w2, w3, turned, o0, o1, o2, o3, split, acc, grams):
    x, core = lax.axis_index("x"), lax.axis_index("c")
    acc[...] = jnp.zeros_like(acc)
    for side, pieces in ((core, (r0, r1, r2, r3)), (1 - core, (w0, w1, w2, w3))):
        for k, piece in enumerate(pieces):
            base = side * 32 + spin(x, k) * 8
            split_all(split, base, piece, 8)
            grams[side * 4 + spin(x, k)] = piece[8]
    multiply(counts[0, 0], cols, rows, turned, split, acc, term_place(lax.axis_index("y")), 16)
    ext = grams[0]
    for i in range(1, 8):
        ext = ext + grams[i]
    for k, out in enumerate((o0, o1, o2, o3)):
        out[0:16] = acc[k * 17 : k * 17 + 16]
        out[16] = ext


def backward(rows, cols, counts, p0, p1, p2, p3, held, own, other, split, acc, grams):
    y = lax.axis_index("y")
    acc[...] = jnp.zeros_like(acc)
    for k, piece in enumerate((p0, p1, p2, p3)):
        base = spin(y, k) * 16
        split_all(split, base, piece, 16)
        grams[spin(y, k)] = piece[16]
    place = doc_place(lax.axis_index("x"), lax.axis_index("c"))
    multiply(counts[0, 0], rows, cols, held, split, acc, place, 8)
    ext = ((grams[0] + grams[1]) + grams[2]) + grams[3]
    for j in range(8):
        acc[j * 9 + 8] = ext
    own[...] = acc[0:36]
    other[...] = acc[36:72]


def left_first(mine, theirs, out, mr0, *, terms):
    inverse = inverse_factor((mine[16] + theirs[16])[:, 0:K] / terms)
    mr0[...] = pad_lanes(inverse)
    cols = columns(inverse)
    gram = jnp.zeros((48, 48), F32)
    for i in range(16):
        value = combine(cols, mine[i] + theirs[i])
        out[i] = value
        wide = stacked(value)
        gram = gram + cross(wide, wide)
    out[16] = pad_lanes(fold(gram))


def zl_total(t0, t1, t2, t3, order):
    zl = lax.axis_index("zl")
    for k, piece in enumerate((t0, t1, t2, t3)):
        order[spin(zl, k)] = piece[...]
    return lambda i: ((order[0, i] + order[1, i]) + order[2, i]) + order[3, i]


def right_first(t0, t1, t2, t3, start, mr0, out, ml1, right0, order, *, docs):
    total = zl_total(t0, t1, t2, t3, order)
    x, core = lax.axis_index("x"), lax.axis_index("c")
    first = (core * 32 + x * 8) * BLK
    inverse = inverse_factor(total(8)[:, 0:K] / docs)
    ml1[...] = pad_lanes(inverse)
    cols_0 = columns(mr0[:, 0:K])
    cols_1 = columns(inverse)
    gram = jnp.zeros((48, 48), F32)
    mixed = jnp.zeros((48, 48), F32)
    for i in range(8):
        source = pl.ds(pl.multiple_of(first + i * BLK, BLK), BLK)
        prior = combine(cols_0, start[:, source])
        right0[i] = prior
        value = combine(cols_1, total(i))
        out[i] = value
        wide = stacked(value)
        gram = gram + cross(wide, wide)
        mixed = mixed + cross(wide, stacked(prior))
    out[8] = pad_lanes(fold(gram), fold(mixed))


def left_second(mine, theirs, left_raw, ml1, out, mr1, h1, *, terms):
    proj, inverse = projected(mine[16] + theirs[16], terms)
    mr1[...] = pad_lanes(inverse)
    h1[...] = pad_lanes(proj)
    cols_l = columns(ml1[:, 0:K])
    cols_h = columns(proj)
    for i in range(16):
        out[i] = (mine[i] + theirs[i]) - combine(cols_h, left_raw[i])
    cols_m = columns(inverse)
    gram = jnp.zeros((48, 48), F32)
    mixed = jnp.zeros((48, 48), F32)
    for i in range(16):
        prior = stacked(combine(cols_l, left_raw[i]))
        value = combine(cols_m, out[i])
        out[i] = value
        wide = stacked(value)
        gram = gram + cross(wide, wide)
        mixed = mixed + cross(wide, prior)
    out[16] = pad_lanes(fold(gram), fold(mixed))


def right_second(t0, t1, t2, t3, right_raw, prior, out, ext_out, ml2, h2, order, *, docs):
    total = zl_total(t0, t1, t2, t3, order)
    first = lax.axis_index("c") * 32 + lax.axis_index("x") * 8
    proj, inverse = projected(total(8), docs)
    ml2[...] = pad_lanes(inverse)
    h2[...] = pad_lanes(proj)
    cols_h = columns(proj)
    for i in range(8):
        out[i] = total(i) - combine(cols_h, right_raw[i])
    cols_m = columns(inverse)
    gram = jnp.zeros((48, 48), F32)
    mixed = jnp.zeros((48, 48), F32)
    for i in range(8):
        value = combine(cols_m, out[i])
        out[i] = value
        wide = stacked(value)
        gram = gram + cross(wide, wide)
        mixed = mixed + cross(wide, prior[first + i])
    both = jnp.concatenate([fold(gram), fold(mixed)], axis=1)
    ext_out[...] = jnp.broadcast_to(
        jnp.concatenate([both[0:8], both[8:16], jnp.zeros((8, 64), F32)], axis=1)[None], (SHARERS, 8, BLK)
    )


def lanes(index):
    return pl.ds(pl.multiple_of(index * BLK, BLK), BLK)


def factor_parts(*matrices):
    tall = [jnp.concatenate([p.astype(F32) for p in parts(m)], axis=0) for m in matrices]
    return jnp.concatenate([t for t in tall for _ in range(3)], axis=1).astype(BF)


def mix(factors, first, second):
    wide = jnp.dot(factors, jnp.concatenate([first, second], axis=0), preferred_element_type=F32)
    return (wide[32:48, :] + wide[16:32, :]) + wide[0:16, :]


def left_result(a0, a1, a2, a3, b0, b1, b2, b3, ml1, ml2, h2, out):
    y = lax.axis_index("y")
    inverse = ml2[:, 0:K]
    factors = factor_parts(inverse, -mm(mm(inverse, h2[:, 0:K]), ml1[:, 0:K]))
    for k, (first, second) in enumerate(zip((a0, a1, a2, a3), (b0, b1, b2, b3))):
        base = spin(y, k) * 16

        def result(i, base=base, first=first, second=second):
            out[:, lanes(base + i)] = mix(factors, stacked(second[i]), stacked(first[i]))

        each(16, result, 8)


def by_side(pieces):
    x, core = lax.axis_index("x"), lax.axis_index("c")
    for n, piece in enumerate(pieces):
        side = core if n < 4 else 1 - core
        yield side * 32 + spin(x, n % 4) * 8, piece


def right_prior(r0, r1, r2, r3, w0, w1, w2, w3, start, mr0, mr1, h1, out, work):
    cols_0 = columns(mr0[:, 0:K])

    def from_start(i):
        work[i] = combine(cols_0, start[:, lanes(i)])

    each(BR, from_start)
    cols_h = columns(h1[:, 0:K])
    for base, piece in by_side((r0, r1, r2, r3, w0, w1, w2, w3)):

        def rest(i, base=base, piece=piece):
            work[base + i] = piece[i] - combine(cols_h, work[base + i])

        each(8, rest)
    cols_1 = columns(mr1[:, 0:K])

    def final(i):
        split_store(out, i, combine(cols_1, work[i]))

    each(BR, final)


def right_result(ext, r0, r1, r2, r3, w0, w1, w2, w3, right1, out, *, terms):
    total = ext[0]
    for i in range(1, SHARERS):
        total = total + ext[i]
    both = jnp.concatenate([total[:, 0 : 2 * K], total[:, 2 * K : 4 * K]], axis=0)
    proj, inverse = projected(both, terms)
    factors = factor_parts(inverse, -mm(inverse, proj))
    for base, piece in by_side((r0, r1, r2, r3, w0, w1, w2, w3)):

        def result(i, base=base, piece=piece):
            out[:, lanes(base + i)] = mix(factors, stacked(piece[i]), right1[base + i])

        each(8, result, 8)


def in_hbm(value):
    return pltpu.with_memory_space_constraint(value, pltpu.HBM)


def panel(n):
    return jax.ShapeDtypeStruct((n, K, BLK), F32)


SMALL = jax.ShapeDtypeStruct((K, BLK), F32)
WIDE = jax.ShapeDtypeStruct((K, BR * BLK), F32)
TILE = jax.ShapeDtypeStruct((NB, BLK, BLK), BF)
SPLIT = VMEM((BR, 48, BLK), BF)


def held_panel(n):
    return VMEM((n, K, BLK), F32)


def call(body, args, outs, scratch=(), spaces=None, limit=8, micros=2, **constants):
    def space(a):
        return SMEM if a.dtype == jnp.int32 else VMEM

    spaces = spaces or [space(a) for a in args]
    return pl.pallas_call(
        functools.partial(body, **constants) if constants else body,
        name=body.__name__,
        out_shape=outs,
        in_specs=[pl.BlockSpec(memory_space=s) for s in spaces],
        out_specs=jax.tree.map(lambda _: pl.BlockSpec(memory_space=VMEM), outs),
        scratch_shapes=list(scratch),
        cost_estimate=pl.CostEstimate(
            flops=micros * 1000000000, bytes_accessed=micros * 1000000, transcendentals=0
        ),
        compiler_params=pltpu.CompilerParams(vmem_limit_bytes=limit * 1024 * 1024),
    )(*args)


SWAP = [(0, 1), (1, 0)]


def shift(value, axis, k):
    return lax.ppermute(value, axis, [(i, (i + k) % 4) for i in range(4)])


def gather(value, axis):
    return [value] + [shift(value, axis, k) for k in (1, 2, 3)]


def total_of(got):
    return ((got[0] + got[1]) + got[2]) + got[3]


def scatter_term(pieces):
    got = [pieces[0]] + [shift(pieces[k], "y", k) for k in (1, 2, 3)]
    mine = total_of(got)
    return mine, lax.ppermute(mine, "zh", SWAP)


def scatter_doc(own, other):
    got = lax.ppermute(other, "c", SWAP)
    pieces = [own[9 * k : 9 * k + 9] + got[9 * k : 9 * k + 9] for k in range(4)]
    got = [pieces[0]] + [shift(pieces[k], "x", k) for k in (1, 2, 3)]
    return gather(total_of(got), "zl")


def gather_doc(value):
    mine = gather(value, "x")
    return mine + [lax.ppermute(m, "c", SWAP) for m in mine]


def local(blocks, block_rows, block_cols, counts, start):
    docs = float(BR * BLK * 32)
    terms = float(BR * BLK * 8)
    index = (block_rows, block_cols, counts)

    *pieces, held, turned = call(
        first_forward,
        (*(in_hbm(v) for v in index[:2]), counts, in_hbm(start), blocks),
        (panel(17),) * 4 + (TILE, TILE),
        [
            SMEM((1, NB), jnp.int32), SMEM((1, NB), jnp.int32), SMEM((1, 1), jnp.int32),
            VMEM((K, BR * BLK), F32), SPLIT, held_panel(68),
            pltpu.SemaphoreType.DMA((NB // GROUP,)), pltpu.SemaphoreType.DMA((4,)),
        ],
        spaces=[pltpu.HBM] * 5,
        limit=30,
    )
    left_chunk, mr0 = call(left_first, scatter_term(pieces), (panel(17), SMALL), terms=terms)
    left1 = gather(left_chunk, "y")
    back_scratch = [SPLIT, held_panel(72), held_panel(4)]
    own, other = call(backward, (*index, *left1, held), (panel(36), panel(36)), back_scratch, limit=20)
    right_chunk, ml1, right0 = call(
        right_first, (*scatter_doc(own, other), start, mr0), (panel(9), SMALL, panel(8)),
        [VMEM((4, 9, K, BLK), F32)], docs=docs,
    )
    right1 = gather_doc(right_chunk)
    pieces = call(
        forward, (*index, *right1, turned), (panel(17),) * 4, [SPLIT, held_panel(68), held_panel(8)], limit=20
    )
    left2_chunk, mr1, h1 = call(
        left_second, (*scatter_term(pieces), left_chunk, ml1), (panel(17), SMALL, SMALL), terms=terms
    )
    left2 = gather(left2_chunk, "y")
    own, other = call(backward, (*index, *left2, held), (panel(36), panel(36)), back_scratch, limit=20)
    prior = call(
        right_prior, (*right1, start, mr0, mr1, h1), jax.ShapeDtypeStruct((BR, 48, BLK), BF), [held_panel(BR)]
    )
    right2_chunk, ext, ml2, h2 = call(
        right_second, (*scatter_doc(own, other), right_chunk, prior),
        (panel(8), jax.ShapeDtypeStruct((SHARERS, 8, BLK), F32), SMALL, SMALL),
        [VMEM((4, 9, K, BLK), F32)], docs=docs,
    )
    mine = gather(right2_chunk, "x")
    ext = lax.all_to_all(ext, ("c", "x", "y", "zh"), 0, 0)
    left_out = call(left_result, (*left1, *left2, ml1, ml2, h2), WIDE)
    mine[3], left_out = lax.optimization_barrier((mine[3], left_out))
    right2 = mine + [lax.ppermute(m, "c", SWAP) for m in mine]
    right_out = call(right_result, (ext, *right2, prior), WIDE, terms=terms)
    return left_out, right_out


def solution(mesh):
    fine = Mesh(np.asarray(mesh.devices).reshape(4, 4, 2, 4, 2), (*DOC, *TERM))
    return jax.shard_map(
        local,
        mesh=fine,
        in_specs=(P(DOC, TERM, None, None), P(DOC, TERM), P(DOC, TERM), P(DOC, TERM), P(None, TERM)),
        out_specs=(P(None, DOC), P(None, TERM)),
        check_vma=False,
    )
```

```python
import functools

import jax
import jax.numpy as jnp
import numpy as np
from jax import lax
from jax.experimental import pallas as pl
from jax.experimental.pallas import tpu as pltpu
from jax.sharding import Mesh
from jax.sharding import PartitionSpec as P

BLK = 128
K = 16
BR = 64
NB = 320
GROUP = 32
SHARERS = 32
AHEAD = 1
DOC = ("zl", "x", "c")
TERM = ("y", "zh")
F32 = jnp.float32
BF = jnp.bfloat16
HI = lax.Precision.HIGHEST
VMEM = pltpu.VMEM
SMEM = pltpu.SMEM
ANY = pl.ANY


def mm(a, b):
    return jnp.dot(a, b, precision=HI, preferred_element_type=F32)


def mmt(a, b):
    return lax.dot_general(a, b, (((1,), (1,)), ((), ())), precision=HI, preferred_element_type=F32)


def inverse_factor(gram):
    lane = lax.broadcasted_iota(jnp.int32, (K, BLK), 1)
    row = lax.broadcasted_iota(jnp.int32, (K, BLK), 0)
    left = columns(gram)
    result = jnp.where(lane == row, 1.0, 0.0)
    scale = jnp.zeros((K, BLK), F32)
    for j in range(K):
        pivot = left[j][j : j + 1, :]
        scale = jnp.where(row == j, lax.rsqrt(pivot), scale)
        if j == K - 1:
            break
        factor = jnp.where(row > j, left[j] * (1.0 / pivot), 0.0)
        result = result - factor * result[j : j + 1, :]
        for k in range(j + 1, K):
            left[k] = left[k] - factor * left[k][j : j + 1, :]
    return (result * scale)[:, 0:K]


def projected(ext, count):
    proj = ext[:, K : 2 * K] / count
    return proj, inverse_factor(ext[:, 0:K] / count - mmt(proj, proj))


def columns(matrix):
    return [jnp.broadcast_to(matrix[:, j : j + 1], (K, BLK)) for j in range(K)]


def combine(cols, piece):
    total = cols[0] * piece[0:1, :]
    for j in range(1, K):
        total = total + cols[j] * piece[j : j + 1, :]
    return total


def parts(value):
    high = value.astype(BF)
    rest = value - high.astype(F32)
    middle = rest.astype(BF)
    low = (rest - middle.astype(F32)).astype(BF)
    return high, middle, low


def stacked(value):
    return jnp.concatenate(parts(value), axis=0)


def split_store(split_ref, index, value):
    high, middle, low = parts(value)
    split_ref[index, 0:16, :] = high
    split_ref[index, 16:32, :] = middle
    split_ref[index, 32:48, :] = low


def each(count, body, unroll=4):
    def step(i, carry):
        body(i)
        return carry

    lax.fori_loop(0, count, step, 0, unroll=unroll)


def split_all(split_ref, base, piece, count):
    each(count, lambda i: split_store(split_ref, base + i, piece[i]), 8)


def cross(left, right):
    return lax.dot_general(left, right, (((1,), (1,)), ((), ())), preferred_element_type=F32)


def fold(wide):
    rows = (wide[32:48, :] + wide[16:32, :]) + wide[0:16, :]
    return (rows[:, 32:48] + rows[:, 16:32]) + rows[:, 0:16]


def pad_lanes(*pieces):
    width = sum(p.shape[1] for p in pieces)
    return jnp.concatenate([*pieces, jnp.zeros((K, BLK - width), F32)], axis=1)


def spin(index, step):
    return jnp.bitwise_and(index - step, 3)


def group_of(base, live, src_ref, tgt_ref, block, split, acc, place, spare):
    spots, values = [], []
    for u in range(GROUP):
        slot = base + u
        wide = jnp.dot(split[src_ref[0, slot]], block(slot), preferred_element_type=F32)
        values.append((wide[32:48, :] + wide[16:32, :]) + wide[0:16, :])
        spots.append(jnp.where(slot < live, place(tgt_ref[0, slot]), spare))
    for spot, value in zip(spots, values):
        acc[spot] += value


def term_place(y):
    def place(target):
        part = jnp.bitwise_and(lax.shift_right_logical(target, 4) - y, 3)
        return part * 17 + jnp.bitwise_and(target, 15)

    return place


def doc_place(x, core):
    def place(target):
        half = jnp.bitwise_xor(lax.shift_right_logical(target, 5), core)
        part = jnp.bitwise_and(lax.shift_right_logical(target, 3) - x, 3)
        return half * 36 + part * 9 + jnp.bitwise_and(target, 7)

    return place


def multiply(live, src_ref, tgt_ref, held, split, acc, place, spare):
    def step(g, carry):
        group_of(g * GROUP, live, src_ref, tgt_ref, lambda s: held[s], split, acc, place, spare)
        return carry

    lax.fori_loop(0, lax.div(live + (GROUP - 1), GROUP), step, 0)


def gram_step(count, value_of, total, unroll=8):
    def step(i, carry):
        value = value_of(i)
        return carry + cross(value, value)

    return lax.fori_loop(0, count, step, total, unroll=unroll)


def first_forward(
    rows_any, cols_any, counts_any, start_any, blocks, o0, o1, o2, o3, held, turned,
    rows, cols, counts, start, split, acc, sems, small_sems,
):
    groups = NB // GROUP
    small = [
        pltpu.make_async_copy(start_any, start, small_sems.at[0]),
        pltpu.make_async_copy(rows_any, rows, small_sems.at[1]),
        pltpu.make_async_copy(cols_any, cols, small_sems.at[2]),
        pltpu.make_async_copy(counts_any, counts, small_sems.at[3]),
    ]
    for copy in small:
        copy.start()
    large = [
        pltpu.make_async_copy(
            blocks.at[0, pl.ds(i * GROUP, GROUP)], held.at[pl.ds(i * GROUP, GROUP)], sems.at[i]
        )
        for i in range(groups)
    ]
    for copy in large[:AHEAD]:
        copy.start()
    acc[...] = jnp.zeros_like(acc)
    for copy in small:
        copy.wait()
    for copy in large[AHEAD:]:
        copy.start()

    def prepare(i):
        value = stacked(start[:, pl.ds(pl.multiple_of(i * BLK, BLK), BLK)])
        split[i] = value
        return value

    ext = pad_lanes(fold(gram_step(BR, prepare, jnp.zeros((48, 48), F32), 16)))
    live = counts[0, 0]
    place = term_place(lax.axis_index("y"))

    def turn(slot):
        value = held[slot].T
        turned[slot] = value
        return value

    def step(i, carry):
        part = pl.ds(i * GROUP, GROUP)
        pltpu.make_async_copy(blocks.at[0, part], held.at[part], sems.at[i]).wait()

        @pl.when(i * GROUP < live)
        def _():
            group_of(i * GROUP, live, cols, rows, turn, split, acc, place, 16)

        return carry

    lax.fori_loop(0, groups, step, 0)
    for k, out in enumerate((o0, o1, o2, o3)):
        out[0:16] = acc[k * 17 : k * 17 + 16]
        out[16] = ext


def forward(rows, cols, counts, r0, r1, r2, r3, w0, w1, w2, w3, turned, o0, o1, o2, o3, split, acc, grams):
    x, core = lax.axis_index("x"), lax.axis_index("c")
    acc[...] = jnp.zeros_like(acc)
    for side, pieces in ((core, (r0, r1, r2, r3)), (1 - core, (w0, w1, w2, w3))):
        for k, piece in enumerate(pieces):
            base = side * 32 + spin(x, k) * 8
            split_all(split, base, piece, 8)
            grams[side * 4 + spin(x, k)] = piece[8]
    multiply(counts[0, 0], cols, rows, turned, split, acc, term_place(lax.axis_index("y")), 16)
    ext = grams[0]
    for i in range(1, 8):
        ext = ext + grams[i]
    for k, out in enumerate((o0, o1, o2, o3)):
        out[0:16] = acc[k * 17 : k * 17 + 16]
        out[16] = ext


def backward(rows, cols, counts, p0, p1, p2, p3, held, own, other, split, acc, grams):
    y = lax.axis_index("y")
    acc[...] = jnp.zeros_like(acc)
    for k, piece in enumerate((p0, p1, p2, p3)):
        base = spin(y, k) * 16
        split_all(split, base, piece, 16)
        grams[spin(y, k)] = piece[16]
    place = doc_place(lax.axis_index("x"), lax.axis_index("c"))
    multiply(counts[0, 0], rows, cols, held, split, acc, place, 8)
    ext = ((grams[0] + grams[1]) + grams[2]) + grams[3]
    for j in range(8):
        acc[j * 9 + 8] = ext
    own[...] = acc[0:36]
    other[...] = acc[36:72]


def left_first(mine, theirs, out, mr0, *, terms):
    inverse = inverse_factor((mine[16] + theirs[16])[:, 0:K] / terms)
    mr0[...] = pad_lanes(inverse)
    cols = columns(inverse)
    gram = jnp.zeros((48, 48), F32)
    for i in range(16):
        value = combine(cols, mine[i] + theirs[i])
        out[i] = value
        wide = stacked(value)
        gram = gram + cross(wide, wide)
    out[16] = pad_lanes(fold(gram))


def zl_total(t0, t1, t2, t3, order):
    zl = lax.axis_index("zl")
    for k, piece in enumerate((t0, t1, t2, t3)):
        order[spin(zl, k)] = piece[...]
    return lambda i: ((order[0, i] + order[1, i]) + order[2, i]) + order[3, i]


def right_first(t0, t1, t2, t3, start, mr0, out, ml1, right0, order, *, docs):
    total = zl_total(t0, t1, t2, t3, order)
    x, core = lax.axis_index("x"), lax.axis_index("c")
    first = (core * 32 + x * 8) * BLK
    inverse = inverse_factor(total(8)[:, 0:K] / docs)
    ml1[...] = pad_lanes(inverse)
    cols_0 = columns(mr0[:, 0:K])
    cols_1 = columns(inverse)
    gram = jnp.zeros((48, 48), F32)
    mixed = jnp.zeros((48, 48), F32)
    for i in range(8):
        source = pl.ds(pl.multiple_of(first + i * BLK, BLK), BLK)
        prior = combine(cols_0, start[:, source])
        right0[i] = prior
        value = combine(cols_1, total(i))
        out[i] = value
        wide = stacked(value)
        gram = gram + cross(wide, wide)
        mixed = mixed + cross(wide, stacked(prior))
    out[8] = pad_lanes(fold(gram), fold(mixed))


def left_second(mine, theirs, left_raw, ml1, out, mr1, h1, *, terms):
    proj, inverse = projected(mine[16] + theirs[16], terms)
    mr1[...] = pad_lanes(inverse)
    h1[...] = pad_lanes(proj)
    cols_l = columns(ml1[:, 0:K])
    cols_h = columns(proj)
    for i in range(16):
        out[i] = (mine[i] + theirs[i]) - combine(cols_h, left_raw[i])
    cols_m = columns(inverse)
    gram = jnp.zeros((48, 48), F32)
    mixed = jnp.zeros((48, 48), F32)
    for i in range(16):
        prior = stacked(combine(cols_l, left_raw[i]))
        value = combine(cols_m, out[i])
        out[i] = value
        wide = stacked(value)
        gram = gram + cross(wide, wide)
        mixed = mixed + cross(wide, prior)
    out[16] = pad_lanes(fold(gram), fold(mixed))


def right_second(t0, t1, t2, t3, right_raw, prior, out, ext_out, ml2, h2, order, *, docs):
    total = zl_total(t0, t1, t2, t3, order)
    first = lax.axis_index("c") * 32 + lax.axis_index("x") * 8
    proj, inverse = projected(total(8), docs)
    ml2[...] = pad_lanes(inverse)
    h2[...] = pad_lanes(proj)
    cols_h = columns(proj)
    for i in range(8):
        out[i] = total(i) - combine(cols_h, right_raw[i])
    cols_m = columns(inverse)
    gram = jnp.zeros((48, 48), F32)
    mixed = jnp.zeros((48, 48), F32)
    for i in range(8):
        value = combine(cols_m, out[i])
        out[i] = value
        wide = stacked(value)
        gram = gram + cross(wide, wide)
        mixed = mixed + cross(wide, prior[first + i])
    both = jnp.concatenate([fold(gram), fold(mixed)], axis=1)
    ext_out[...] = jnp.concatenate([both[0:8], both[8:16], jnp.zeros((8, BLK - 4 * K), F32)], axis=1)


def lanes(index):
    return pl.ds(pl.multiple_of(index * BLK, BLK), BLK)


def factor_parts(*matrices):
    tall = [jnp.concatenate([p.astype(F32) for p in parts(m)], axis=0) for m in matrices]
    return jnp.concatenate([t for t in tall for _ in range(3)], axis=1).astype(BF)


def mix(factors, first, second):
    wide = jnp.dot(factors, jnp.concatenate([first, second], axis=0), preferred_element_type=F32)
    return (wide[32:48, :] + wide[16:32, :]) + wide[0:16, :]


def left_result(a0, a1, a2, a3, b0, b1, b2, b3, ml1, ml2, h2, out):
    y = lax.axis_index("y")
    inverse = ml2[:, 0:K]
    factors = factor_parts(inverse, -mm(mm(inverse, h2[:, 0:K]), ml1[:, 0:K]))
    for k, (first, second) in enumerate(zip((a0, a1, a2, a3), (b0, b1, b2, b3))):
        base = spin(y, k) * 16

        def result(i, base=base, first=first, second=second):
            out[:, lanes(base + i)] = mix(factors, stacked(second[i]), stacked(first[i]))

        each(16, result, 8)


def by_side(pieces):
    x, core = lax.axis_index("x"), lax.axis_index("c")
    for n, piece in enumerate(pieces):
        side = core if n < 4 else 1 - core
        yield side * 32 + spin(x, n % 4) * 8, piece


def right_prior(r0, r1, r2, r3, w0, w1, w2, w3, start, mr0, mr1, h1, out, work):
    cols_0 = columns(mr0[:, 0:K])

    def from_start(i):
        work[i] = combine(cols_0, start[:, lanes(i)])

    each(BR, from_start)
    cols_h = columns(h1[:, 0:K])
    for base, piece in by_side((r0, r1, r2, r3, w0, w1, w2, w3)):

        def rest(i, base=base, piece=piece):
            work[base + i] = piece[i] - combine(cols_h, work[base + i])

        each(8, rest)
    cols_1 = columns(mr1[:, 0:K])

    def final(i):
        split_store(out, i, combine(cols_1, work[i]))

    each(BR, final)


def right_result(ext, r0, r1, r2, r3, w0, w1, w2, w3, right1, out, *, terms):
    total = ext[0]
    for i in range(1, SHARERS):
        total = total + ext[i]
    both = jnp.concatenate([total[:, 0 : 2 * K], total[:, 2 * K : 4 * K]], axis=0)
    proj, inverse = projected(both, terms)
    factors = factor_parts(inverse, -mm(inverse, proj))
    for base, piece in by_side((r0, r1, r2, r3, w0, w1, w2, w3)):

        def result(i, base=base, piece=piece):
            out[:, lanes(base + i)] = mix(factors, stacked(piece[i]), right1[base + i])

        each(8, result, 8)


def in_hbm(value):
    return pltpu.with_memory_space_constraint(value, pltpu.HBM)


def panel(n):
    return jax.ShapeDtypeStruct((n, K, BLK), F32)


SMALL = jax.ShapeDtypeStruct((K, BLK), F32)
WIDE = jax.ShapeDtypeStruct((K, BR * BLK), F32)
TILE = jax.ShapeDtypeStruct((NB, BLK, BLK), BF)
SPLIT = VMEM((BR, 48, BLK), BF)


def held_panel(n):
    return VMEM((n, K, BLK), F32)


def call(body, args, outs, scratch=(), spaces=None, limit=8, micros=2, **constants):
    def space(a):
        return SMEM if a.dtype == jnp.int32 else VMEM

    spaces = spaces or [space(a) for a in args]
    return pl.pallas_call(
        functools.partial(body, **constants) if constants else body,
        name=body.__name__,
        out_shape=outs,
        in_specs=[pl.BlockSpec(memory_space=s) for s in spaces],
        out_specs=jax.tree.map(lambda _: pl.BlockSpec(memory_space=VMEM), outs),
        scratch_shapes=list(scratch),
        cost_estimate=pl.CostEstimate(
            flops=micros * 1000000000, bytes_accessed=micros * 1000000, transcendentals=0
        ),
        compiler_params=pltpu.CompilerParams(vmem_limit_bytes=limit * 1024 * 1024),
    )(*args)


SWAP = [(0, 1), (1, 0)]


def shift(value, axis, k):
    return lax.ppermute(value, axis, [(i, (i + k) % 4) for i in range(4)])


def gather(value, axis):
    return [value] + [shift(value, axis, k) for k in (1, 2, 3)]


def total_of(got):
    return ((got[0] + got[1]) + got[2]) + got[3]


def scatter_term(pieces):
    got = [pieces[0]] + [shift(pieces[k], "y", k) for k in (1, 2, 3)]
    mine = total_of(got)
    return mine, lax.ppermute(mine, "zh", SWAP)


def scatter_doc(own, other):
    got = lax.ppermute(other, "c", SWAP)
    pieces = [own[9 * k : 9 * k + 9] + got[9 * k : 9 * k + 9] for k in range(4)]
    got = [pieces[0]] + [shift(pieces[k], "x", k) for k in (1, 2, 3)]
    return gather(total_of(got), "zl")


def gather_doc(value):
    mine = gather(value, "x")
    return mine + [lax.ppermute(m, "c", SWAP) for m in mine]


def local(blocks, block_rows, block_cols, counts, start):
    docs = float(BR * BLK * 32)
    terms = float(BR * BLK * 8)
    index = (block_rows, block_cols, counts)

    *pieces, held, turned = call(
        first_forward,
        (*(in_hbm(v) for v in index[:2]), counts, in_hbm(start), blocks),
        (panel(17),) * 4 + (TILE, TILE),
        [
            SMEM((1, NB), jnp.int32), SMEM((1, NB), jnp.int32), SMEM((1, 1), jnp.int32),
            VMEM((K, BR * BLK), F32), SPLIT, held_panel(68),
            pltpu.SemaphoreType.DMA((NB // GROUP,)), pltpu.SemaphoreType.DMA((4,)),
        ],
        spaces=[pltpu.HBM] * 5,
        limit=30,
    )
    left_chunk, mr0 = call(left_first, scatter_term(pieces), (panel(17), SMALL), terms=terms)
    left1 = gather(left_chunk, "y")
    back_scratch = [SPLIT, held_panel(72), held_panel(4)]
    own, other = call(backward, (*index, *left1, held), (panel(36), panel(36)), back_scratch, limit=20)
    right_chunk, ml1, right0 = call(
        right_first, (*scatter_doc(own, other), start, mr0), (panel(9), SMALL, panel(8)),
        [VMEM((4, 9, K, BLK), F32)], docs=docs,
    )
    right1 = gather_doc(right_chunk)
    pieces = call(
        forward, (*index, *right1, turned), (panel(17),) * 4, [SPLIT, held_panel(68), held_panel(8)], limit=20
    )
    left2_chunk, mr1, h1 = call(
        left_second, (*scatter_term(pieces), left_chunk, ml1), (panel(17), SMALL, SMALL), terms=terms
    )
    left2 = gather(left2_chunk, "y")
    own, other = call(backward, (*index, *left2, held), (panel(36), panel(36)), back_scratch, limit=20)
    prior = call(
        right_prior, (*right1, start, mr0, mr1, h1), jax.ShapeDtypeStruct((BR, 48, BLK), BF), [held_panel(BR)]
    )
    right2_chunk, ext, ml2, h2 = call(
        right_second, (*scatter_doc(own, other), right_chunk, prior),
        (panel(8), jax.ShapeDtypeStruct((8, BLK), F32), SMALL, SMALL),
        [VMEM((4, 9, K, BLK), F32)], docs=docs,
    )
    mine = gather(right2_chunk, "x")
    left_out = call(left_result, (*left1, *left2, ml1, ml2, h2), WIDE)
    ext = ext + lax.ppermute(ext, "zh", SWAP)
    ext, left_out, *mine = lax.optimization_barrier((ext, left_out, *mine))
    ext = lax.all_to_all(jnp.broadcast_to(ext[None], (SHARERS, 8, BLK)), ("c", "x", "y"), 0, 0)
    right2 = mine + [lax.ppermute(m, "c", SWAP) for m in mine]
    right_out = call(right_result, (ext, *right2, prior), WIDE, terms=terms)
    return left_out, right_out


def solution(mesh):
    fine = Mesh(np.asarray(mesh.devices).reshape(4, 4, 2, 4, 2), (*DOC, *TERM))
    return jax.shard_map(
        local,
        mesh=fine,
        in_specs=(P(DOC, TERM, None, None), P(DOC, TERM), P(DOC, TERM), P(DOC, TERM), P(None, TERM)),
        out_specs=(P(None, DOC), P(None, TERM)),
        check_vma=False,
    )
```

```python
import functools

import jax
import jax.numpy as jnp
import numpy as np
from jax import lax
from jax.experimental import pallas as pl
from jax.experimental.pallas import tpu as pltpu
from jax.sharding import Mesh
from jax.sharding import PartitionSpec as P

BLK = 128
K = 16
BR = 64
NB = 320
GROUP = 32
WIDER = 64
SHARERS = 32
AHEAD = 1
DOC = ("zl", "x", "c")
TERM = ("y", "zh")
F32 = jnp.float32
BF = jnp.bfloat16
HI = lax.Precision.HIGHEST
VMEM = pltpu.VMEM
SMEM = pltpu.SMEM
ANY = pl.ANY


def mm(a, b):
    return jnp.dot(a, b, precision=HI, preferred_element_type=F32)


def mmt(a, b):
    return lax.dot_general(a, b, (((1,), (1,)), ((), ())), precision=HI, preferred_element_type=F32)


def inverse_factor(gram):
    lane = lax.broadcasted_iota(jnp.int32, (K, BLK), 1)
    row = lax.broadcasted_iota(jnp.int32, (K, BLK), 0)
    left = columns(gram)
    result = jnp.where(lane == row, 1.0, 0.0)
    scale = jnp.zeros((K, BLK), F32)
    for j in range(K):
        pivot = left[j][j : j + 1, :]
        scale = jnp.where(row == j, lax.rsqrt(pivot), scale)
        if j == K - 1:
            break
        factor = jnp.where(row > j, left[j] * (1.0 / pivot), 0.0)
        result = result - factor * result[j : j + 1, :]
        for k in range(j + 1, K):
            left[k] = left[k] - factor * left[k][j : j + 1, :]
    return (result * scale)[:, 0:K]


def projected(ext, count):
    proj = ext[:, K : 2 * K] / count
    return proj, inverse_factor(ext[:, 0:K] / count - mmt(proj, proj))


def columns(matrix):
    return [jnp.broadcast_to(matrix[:, j : j + 1], (K, BLK)) for j in range(K)]


def combine(cols, piece):
    total = cols[0] * piece[0:1, :]
    for j in range(1, K):
        total = total + cols[j] * piece[j : j + 1, :]
    return total


def parts(value):
    high = value.astype(BF)
    rest = value - high.astype(F32)
    middle = rest.astype(BF)
    low = (rest - middle.astype(F32)).astype(BF)
    return high, middle, low


def stacked(value):
    return jnp.concatenate(parts(value), axis=0)


def split_store(split_ref, index, value):
    high, middle, low = parts(value)
    split_ref[index, 0:16, :] = high
    split_ref[index, 16:32, :] = middle
    split_ref[index, 32:48, :] = low


def each(count, body, unroll=2):
    def step(i, carry):
        body(i)
        return carry

    lax.fori_loop(0, count, step, 0, unroll=unroll)


def split_all(split_ref, base, piece, count):
    each(count, lambda i: split_store(split_ref, base + i, piece[i]), 4)


def cross(left, right):
    return lax.dot_general(left, right, (((1,), (1,)), ((), ())), preferred_element_type=F32)


def fold(wide):
    rows = (wide[32:48, :] + wide[16:32, :]) + wide[0:16, :]
    return (rows[:, 32:48] + rows[:, 16:32]) + rows[:, 0:16]


def pad_lanes(*pieces):
    width = sum(p.shape[1] for p in pieces)
    return jnp.concatenate([*pieces, jnp.zeros((K, BLK - width), F32)], axis=1)


def spin(index, step):
    return jnp.bitwise_and(index - step, 3)


def group_of(size, base, live, src_ref, tgt_ref, block, split, acc, place, spare):
    spots, values = [], []
    for u in range(size):
        slot = base + u
        wide = jnp.dot(split[src_ref[0, slot]], block(slot), preferred_element_type=F32)
        values.append((wide[32:48, :] + wide[16:32, :]) + wide[0:16, :])
        spots.append(jnp.where(slot < live, place(tgt_ref[0, slot]), spare))
    for spot, value in zip(spots, values):
        acc[spot] += value


def term_place(y):
    def place(target):
        part = jnp.bitwise_and(lax.shift_right_logical(target, 4) - y, 3)
        return part * 17 + jnp.bitwise_and(target, 15)

    return place


def doc_place(x, core):
    def place(target):
        half = jnp.bitwise_xor(lax.shift_right_logical(target, 5), core)
        part = jnp.bitwise_and(lax.shift_right_logical(target, 3) - x, 3)
        return half * 36 + part * 9 + jnp.bitwise_and(target, 7)

    return place


def multiply(live, src_ref, tgt_ref, held, split, acc, place, spare):
    def step(g, carry):
        group_of(WIDER, g * WIDER, live, src_ref, tgt_ref, lambda s: held[s], split, acc, place, spare)
        return carry

    lax.fori_loop(0, lax.div(live + (WIDER - 1), WIDER), step, 0)


def gram_step(count, value_of, total, unroll=8):
    def step(i, carry):
        value = value_of(i)
        return carry + cross(value, value)

    return lax.fori_loop(0, count, step, total, unroll=unroll)


def first_forward(
    rows_any, cols_any, counts_any, start_any, blocks, o0, o1, o2, o3, held, turned,
    rows, cols, counts, start, split, acc, sems, small_sems,
):
    groups = NB // GROUP
    small = [
        pltpu.make_async_copy(start_any, start, small_sems.at[0]),
        pltpu.make_async_copy(rows_any, rows, small_sems.at[1]),
        pltpu.make_async_copy(cols_any, cols, small_sems.at[2]),
        pltpu.make_async_copy(counts_any, counts, small_sems.at[3]),
    ]
    for copy in small:
        copy.start()
    large = [
        pltpu.make_async_copy(
            blocks.at[0, pl.ds(i * GROUP, GROUP)], held.at[pl.ds(i * GROUP, GROUP)], sems.at[i]
        )
        for i in range(groups)
    ]
    for copy in large[:AHEAD]:
        copy.start()
    acc[...] = jnp.zeros_like(acc)
    for copy in small:
        copy.wait()
    for copy in large[AHEAD:]:
        copy.start()

    def prepare(i):
        value = stacked(start[:, pl.ds(pl.multiple_of(i * BLK, BLK), BLK)])
        split[i] = value
        return value

    ext = pad_lanes(fold(gram_step(BR, prepare, jnp.zeros((48, 48), F32), 8)))
    live = counts[0, 0]
    place = term_place(lax.axis_index("y"))

    def turn(slot):
        value = held[slot].T
        turned[slot] = value
        return value

    def step(i, carry):
        part = pl.ds(i * GROUP, GROUP)
        pltpu.make_async_copy(blocks.at[0, part], held.at[part], sems.at[i]).wait()

        @pl.when(i * GROUP < live)
        def _():
            group_of(GROUP, i * GROUP, live, cols, rows, turn, split, acc, place, 16)

        return carry

    lax.fori_loop(0, groups, step, 0)
    for k, out in enumerate((o0, o1, o2, o3)):
        out[0:16] = acc[k * 17 : k * 17 + 16]
        out[16] = ext


def forward(rows, cols, counts, r0, r1, r2, r3, w0, w1, w2, w3, turned, o0, o1, o2, o3, split, acc, grams):
    x, core = lax.axis_index("x"), lax.axis_index("c")
    acc[...] = jnp.zeros_like(acc)
    for side, pieces in ((core, (r0, r1, r2, r3)), (1 - core, (w0, w1, w2, w3))):
        for k, piece in enumerate(pieces):
            base = side * 32 + spin(x, k) * 8
            split_all(split, base, piece, 8)
            grams[side * 4 + spin(x, k)] = piece[8]
    multiply(counts[0, 0], cols, rows, turned, split, acc, term_place(lax.axis_index("y")), 16)
    ext = grams[0]
    for i in range(1, 8):
        ext = ext + grams[i]
    for k, out in enumerate((o0, o1, o2, o3)):
        out[0:16] = acc[k * 17 : k * 17 + 16]
        out[16] = ext


def backward(rows, cols, counts, p0, p1, p2, p3, held, own, other, split, acc, grams):
    y = lax.axis_index("y")
    acc[...] = jnp.zeros_like(acc)
    for k, piece in enumerate((p0, p1, p2, p3)):
        base = spin(y, k) * 16
        split_all(split, base, piece, 16)
        grams[spin(y, k)] = piece[16]
    place = doc_place(lax.axis_index("x"), lax.axis_index("c"))
    multiply(counts[0, 0], rows, cols, held, split, acc, place, 8)
    ext = ((grams[0] + grams[1]) + grams[2]) + grams[3]
    for j in range(8):
        acc[j * 9 + 8] = ext
    own[...] = acc[0:36]
    other[...] = acc[36:72]


def left_first(mine, theirs, out, mr0, *, terms):
    inverse = inverse_factor((mine[16] + theirs[16])[:, 0:K] / terms)
    mr0[...] = pad_lanes(inverse)
    cols = columns(inverse)
    gram = jnp.zeros((48, 48), F32)
    for i in range(16):
        value = combine(cols, mine[i] + theirs[i])
        out[i] = value
        wide = stacked(value)
        gram = gram + cross(wide, wide)
    out[16] = pad_lanes(fold(gram))


def zl_total(t0, t1, t2, t3, order):
    zl = lax.axis_index("zl")
    for k, piece in enumerate((t0, t1, t2, t3)):
        order[spin(zl, k)] = piece[...]
    return lambda i: ((order[0, i] + order[1, i]) + order[2, i]) + order[3, i]


def right_first(t0, t1, t2, t3, start, mr0, out, ml1, right0, order, *, docs):
    total = zl_total(t0, t1, t2, t3, order)
    x, core = lax.axis_index("x"), lax.axis_index("c")
    first = (core * 32 + x * 8) * BLK
    inverse = inverse_factor(total(8)[:, 0:K] / docs)
    ml1[...] = pad_lanes(inverse)
    cols_0 = columns(mr0[:, 0:K])
    cols_1 = columns(inverse)
    gram = jnp.zeros((48, 48), F32)
    mixed = jnp.zeros((48, 48), F32)
    for i in range(8):
        source = pl.ds(pl.multiple_of(first + i * BLK, BLK), BLK)
        prior = combine(cols_0, start[:, source])
        right0[i] = prior
        value = combine(cols_1, total(i))
        out[i] = value
        wide = stacked(value)
        gram = gram + cross(wide, wide)
        mixed = mixed + cross(wide, stacked(prior))
    out[8] = pad_lanes(fold(gram), fold(mixed))


def left_second(mine, theirs, left_raw, ml1, out, mr1, h1, *, terms):
    proj, inverse = projected(mine[16] + theirs[16], terms)
    mr1[...] = pad_lanes(inverse)
    h1[...] = pad_lanes(proj)
    cols_l = columns(ml1[:, 0:K])
    cols_h = columns(proj)
    for i in range(16):
        out[i] = (mine[i] + theirs[i]) - combine(cols_h, left_raw[i])
    cols_m = columns(inverse)
    gram = jnp.zeros((48, 48), F32)
    mixed = jnp.zeros((48, 48), F32)
    for i in range(16):
        prior = stacked(combine(cols_l, left_raw[i]))
        value = combine(cols_m, out[i])
        out[i] = value
        wide = stacked(value)
        gram = gram + cross(wide, wide)
        mixed = mixed + cross(wide, prior)
    out[16] = pad_lanes(fold(gram), fold(mixed))


def right_second(t0, t1, t2, t3, right_raw, prior, out, ext_out, ml2, h2, order, *, docs):
    total = zl_total(t0, t1, t2, t3, order)
    first = lax.axis_index("c") * 32 + lax.axis_index("x") * 8
    proj, inverse = projected(total(8), docs)
    ml2[...] = pad_lanes(inverse)
    h2[...] = pad_lanes(proj)
    cols_h = columns(proj)
    for i in range(8):
        out[i] = total(i) - combine(cols_h, right_raw[i])
    cols_m = columns(inverse)
    gram = jnp.zeros((48, 48), F32)
    mixed = jnp.zeros((48, 48), F32)
    for i in range(8):
        value = combine(cols_m, out[i])
        out[i] = value
        wide = stacked(value)
        gram = gram + cross(wide, wide)
        mixed = mixed + cross(wide, prior[first + i])
    both = jnp.concatenate([fold(gram), fold(mixed)], axis=1)
    ext_out[...] = jnp.concatenate([both[0:8], both[8:16], jnp.zeros((8, BLK - 4 * K), F32)], axis=1)


def lanes(index):
    return pl.ds(pl.multiple_of(index * BLK, BLK), BLK)


def factor_parts(*matrices):
    tall = [jnp.concatenate([p.astype(F32) for p in parts(m)], axis=0) for m in matrices]
    return jnp.concatenate([t for t in tall for _ in range(3)], axis=1).astype(BF)


def mix(factors, first, second):
    wide = jnp.dot(factors, jnp.concatenate([first, second], axis=0), preferred_element_type=F32)
    return (wide[32:48, :] + wide[16:32, :]) + wide[0:16, :]


def left_result(a0, a1, a2, a3, b0, b1, b2, b3, ml1, ml2, h2, out):
    y = lax.axis_index("y")
    inverse = ml2[:, 0:K]
    factors = factor_parts(inverse, -mm(mm(inverse, h2[:, 0:K]), ml1[:, 0:K]))
    for k, (first, second) in enumerate(zip((a0, a1, a2, a3), (b0, b1, b2, b3))):
        base = spin(y, k) * 16

        def result(i, base=base, first=first, second=second):
            out[:, lanes(base + i)] = mix(factors, stacked(second[i]), stacked(first[i]))

        each(16, result, 4)


def by_side(pieces):
    x, core = lax.axis_index("x"), lax.axis_index("c")
    for n, piece in enumerate(pieces):
        side = core if n < 4 else 1 - core
        yield side * 32 + spin(x, n % 4) * 8, piece


def right_prior(r0, r1, r2, r3, w0, w1, w2, w3, start, mr0, mr1, h1, out, work):
    cols_0 = columns(mr0[:, 0:K])

    def from_start(i):
        work[i] = combine(cols_0, start[:, lanes(i)])

    each(BR, from_start)
    cols_h = columns(h1[:, 0:K])
    for base, piece in by_side((r0, r1, r2, r3, w0, w1, w2, w3)):

        def rest(i, base=base, piece=piece):
            work[base + i] = piece[i] - combine(cols_h, work[base + i])

        each(8, rest)
    cols_1 = columns(mr1[:, 0:K])

    def final(i):
        split_store(out, i, combine(cols_1, work[i]))

    each(BR, final)


def right_result(ext, r0, r1, r2, r3, w0, w1, w2, w3, right1, out, *, terms):
    total = ext[0]
    for i in range(1, SHARERS):
        total = total + ext[i]
    both = jnp.concatenate([total[:, 0 : 2 * K], total[:, 2 * K : 4 * K]], axis=0)
    proj, inverse = projected(both, terms)
    factors = factor_parts(inverse, -mm(inverse, proj))
    for base, piece in by_side((r0, r1, r2, r3, w0, w1, w2, w3)):

        def result(i, base=base, piece=piece):
            out[:, lanes(base + i)] = mix(factors, stacked(piece[i]), right1[base + i])

        each(8, result, 8)


def in_hbm(value):
    return pltpu.with_memory_space_constraint(value, pltpu.HBM)


def panel(n):
    return jax.ShapeDtypeStruct((n, K, BLK), F32)


SMALL = jax.ShapeDtypeStruct((K, BLK), F32)
WIDE = jax.ShapeDtypeStruct((K, BR * BLK), F32)
TILE = jax.ShapeDtypeStruct((NB, BLK, BLK), BF)
SPLIT = VMEM((BR, 48, BLK), BF)


def held_panel(n):
    return VMEM((n, K, BLK), F32)


def call(body, args, outs, scratch=(), spaces=None, limit=8, micros=2, **constants):
    def space(a):
        return SMEM if a.dtype == jnp.int32 else VMEM

    spaces = spaces or [space(a) for a in args]
    return pl.pallas_call(
        functools.partial(body, **constants) if constants else body,
        name=body.__name__,
        out_shape=outs,
        in_specs=[pl.BlockSpec(memory_space=s) for s in spaces],
        out_specs=jax.tree.map(lambda _: pl.BlockSpec(memory_space=VMEM), outs),
        scratch_shapes=list(scratch),
        cost_estimate=pl.CostEstimate(
            flops=micros * 1000000000, bytes_accessed=micros * 1000000, transcendentals=0
        ),
        compiler_params=pltpu.CompilerParams(vmem_limit_bytes=limit * 1024 * 1024),
    )(*args)


SWAP = [(0, 1), (1, 0)]


def shift(value, axis, k):
    return lax.ppermute(value, axis, [(i, (i + k) % 4) for i in range(4)])


def gather(value, axis):
    return [value] + [shift(value, axis, k) for k in (1, 2, 3)]


def total_of(got):
    return ((got[0] + got[1]) + got[2]) + got[3]


def scatter_term(pieces):
    got = [pieces[0]] + [shift(pieces[k], "y", k) for k in (1, 2, 3)]
    mine = total_of(got)
    return mine, lax.ppermute(mine, "zh", SWAP)


def scatter_doc(own, other):
    got = lax.ppermute(other, "c", SWAP)
    pieces = [own[9 * k : 9 * k + 9] + got[9 * k : 9 * k + 9] for k in range(4)]
    got = [pieces[0]] + [shift(pieces[k], "x", k) for k in (1, 2, 3)]
    return gather(total_of(got), "zl")


def gather_doc(value):
    mine = gather(value, "x")
    return mine + [lax.ppermute(m, "c", SWAP) for m in mine]


def local(blocks, block_rows, block_cols, counts, start):
    docs = float(BR * BLK * 32)
    terms = float(BR * BLK * 8)
    index = (block_rows, block_cols, counts)

    *pieces, held, turned = call(
        first_forward,
        (*(in_hbm(v) for v in index[:2]), counts, in_hbm(start), blocks),
        (panel(17),) * 4 + (TILE, TILE),
        [
            SMEM((1, NB), jnp.int32), SMEM((1, NB), jnp.int32), SMEM((1, 1), jnp.int32),
            VMEM((K, BR * BLK), F32), SPLIT, held_panel(68),
            pltpu.SemaphoreType.DMA((NB // GROUP,)), pltpu.SemaphoreType.DMA((4,)),
        ],
        spaces=[pltpu.HBM] * 5,
        limit=30,
    )
    left_chunk, mr0 = call(left_first, scatter_term(pieces), (panel(17), SMALL), terms=terms)
    left1 = gather(left_chunk, "y")
    back_scratch = [SPLIT, held_panel(72), held_panel(4)]
    own, other = call(backward, (*index, *left1, held), (panel(36), panel(36)), back_scratch, limit=20)
    right_chunk, ml1, right0 = call(
        right_first, (*scatter_doc(own, other), start, mr0), (panel(9), SMALL, panel(8)),
        [VMEM((4, 9, K, BLK), F32)], docs=docs,
    )
    right1 = gather_doc(right_chunk)
    pieces = call(
        forward, (*index, *right1, turned), (panel(17),) * 4, [SPLIT, held_panel(68), held_panel(8)], limit=20
    )
    left2_chunk, mr1, h1 = call(
        left_second, (*scatter_term(pieces), left_chunk, ml1), (panel(17), SMALL, SMALL), terms=terms
    )
    left2 = gather(left2_chunk, "y")
    own, other = call(backward, (*index, *left2, held), (panel(36), panel(36)), back_scratch, limit=20)
    prior = call(
        right_prior, (*right1, start, mr0, mr1, h1), jax.ShapeDtypeStruct((BR, 48, BLK), BF), [held_panel(BR)]
    )
    right2_chunk, ext, ml2, h2 = call(
        right_second, (*scatter_doc(own, other), right_chunk, prior),
        (panel(8), jax.ShapeDtypeStruct((8, BLK), F32), SMALL, SMALL),
        [VMEM((4, 9, K, BLK), F32)], docs=docs,
    )
    mine = gather(right2_chunk, "x")
    left_out = call(left_result, (*left1, *left2, ml1, ml2, h2), WIDE)
    ext = ext + lax.ppermute(ext, "zh", SWAP)
    ext, left_out, *mine = lax.optimization_barrier((ext, left_out, *mine))
    ext = lax.all_to_all(jnp.broadcast_to(ext[None], (SHARERS, 8, BLK)), ("c", "x", "y"), 0, 0)
    right2 = mine + [lax.ppermute(m, "c", SWAP) for m in mine]
    right_out = call(right_result, (ext, *right2, prior), WIDE, terms=terms)
    return left_out, right_out


def solution(mesh):
    fine = Mesh(np.asarray(mesh.devices).reshape(4, 4, 2, 4, 2), (*DOC, *TERM))
    return jax.shard_map(
        local,
        mesh=fine,
        in_specs=(P(DOC, TERM, None, None), P(DOC, TERM), P(DOC, TERM), P(DOC, TERM), P(None, TERM)),
        out_specs=(P(None, DOC), P(None, TERM)),
        check_vma=False,
    )
```
